32 devices in a mesh: shot: 8 (over z, x), line: 4 (over y, core).
Axes of the slice: x: 2, y: 2, z: 4, core: 2. Of those that a mesh axis runs over, the one named last changes fastest.
Arguments:
- traces: bfloat16 [16384, 2048], P(('shot', 'line')), may hold values from -12 to 12
- targets: bfloat16 [16384, 2048], P(('shot', 'line')), may hold values from -64 to 64
- src_local: int32 [16384], P(('shot', 'line')), may hold values from 0 to 3
- rcv_term: int32 [16384], P(('shot', 'line')), may hold values from 0 to 4095, as said below
- cmp_term: int32 [16384], P(('shot', 'line')), may hold values from 0 to 8191, as said below
- rcv_home: int32 [4096], replicated, may hold values from 0 to 4095, as said below
- cmp_home: int32 [8192], replicated, may hold values from 0 to 8191, as said below
- counts: int32 [32], P(('shot', 'line')), may hold values from 128 to 512, as said below
- src_filters: float32 [128, 128], P(('shot', 'line')), may hold values from -1.75 to 1.75
- rcv_filters: float32 [4096, 128], P(('shot', 'line')), may hold values from -1.75 to 1.75
- cmp_filters: float32 [8192, 128], P(('shot', 'line')), may hold values from -1.75 to 1.75
Outputs:
- src_out: float32 [128, 128], P(('shot', 'line'))
- rcv_out: float32 [4096, 128], P(('shot', 'line'))
- cmp_out: float32 [8192, 128], P(('shot', 'line'))
The draws below stay inside these ranges and needn't reach their ends.
Inputs may be any that keep to these rules, and one draw needn't show every extreme that they name: Receiver row rcv_home[rcv_term[t]] lies on device rcv_home[rcv_term[t]] // 128. Among the 512 trace slots of one device (live or not) at most 32 have receiver rows on any one device; in every draw some device holds the receiver rows of exactly 32 slots of every device. `cmp_term`: likewise for CMP rows with 256 rows a device: at most 32 slots of one device name CMP rows on any one device, and some device is named so by exactly 32 slots of every device. `rcv_home`: A permutation of 0 to 4095. `cmp_home`: A permutation of 0 to 8191. The first counts[d] slots of device d are live; some device is full.
All inputs are finite; a program needn't handle non-finite values.
Results may differ from the reference program's by a relative error of at most 0.0027.
Values sent between devices are 32-bit elements; how exact they have to be, the bound alone decides.
A program may use at most 64 MiB of HBM per device.

```python
import jax
import jax.numpy as jnp
from jax import lax

TAPS = 128
NS = 2048
TR_DEV = 512
SRC_DEV = 4
RCV_DEV = 128
CMP_DEV = 256
TRACES = 16384
NSRC = 128
NRCV = 4096
NCMP = 8192
CAP = 32
DEVICES = 32


def owner_slots(key, terms_dev):
    star_key, rest_key, place_key = jax.random.split(key, 3)
    star_owner = jax.random.randint(star_key, (), 0, DEVICES).astype(jnp.int32)

    def one_device(device_key):
        first_key, second_key = jax.random.split(device_key)
        others = (jnp.arange(CAP * (DEVICES - 1), dtype=jnp.int32) // CAP + star_owner + 1) % DEVICES
        others = jax.random.permutation(first_key, others)[:TR_DEV - CAP]
        owners = jnp.concatenate([jnp.full((CAP,), star_owner, jnp.int32), others.astype(jnp.int32)])
        return jax.random.permutation(second_key, owners)
    device_keys = jax.random.split(rest_key, DEVICES)
    owners = jax.vmap(one_device)(device_keys)
    place_rows = jax.random.randint(place_key, (DEVICES, TR_DEV), 0, terms_dev).astype(jnp.int32)
    return (owners * terms_dev + place_rows).reshape(-1).astype(jnp.int32)


def term_tables(key, salt, terms_dev, term_total):
    slot_rows = owner_slots(jax.random.fold_in(key, salt), terms_dev)
    home_rows = jax.random.permutation(jax.random.fold_in(key, salt + 1), term_total).astype(jnp.int32)
    inverse = jnp.argsort(home_rows).astype(jnp.int32)
    return (inverse[slot_rows].astype(jnp.int32), home_rows)


def draw_rcv_term(key, part):
    shared = term_tables(key, 101, RCV_DEV, NRCV)
    return shared[0]


def draw_rcv_home(key, part):
    shared = term_tables(key, 101, RCV_DEV, NRCV)
    return shared[1]


def draw_cmp_term(key, part):
    shared = term_tables(key, 201, CMP_DEV, NCMP)
    return shared[0]


def draw_cmp_home(key, part):
    shared = term_tables(key, 201, CMP_DEV, NCMP)
    return shared[1]


def draw_counts(key, part):
    key = jax.random.fold_in(key, 7)
    first_key, second_key = jax.random.split(key)
    counts = jax.random.randint(first_key, (DEVICES,), TR_DEV // 4, TR_DEV + 1)
    full_device = jax.random.randint(second_key, (), 0, DEVICES)
    return jnp.where(jnp.arange(DEVICES) == full_device, TR_DEV, counts).astype(jnp.int32)


def draw_traces(key, part):
    key = jax.random.fold_in(key, 11)
    first_key, second_key = jax.random.split(key)
    base_draw = jax.random.truncated_normal(first_key, -4.0, 4.0, (TRACES, NS), jnp.float32)
    row_scale = jnp.exp(jax.random.uniform(second_key, (TRACES, 1), jnp.float32, jnp.log(0.3), jnp.log(3.0)))
    return (base_draw * row_scale).astype(jnp.bfloat16)


def set_ends(array, rng, low, top_value):
    spot = [jax.random.randint(jax.random.fold_in(rng, axis), (), 0, length) for axis, length in enumerate(array.shape)]
    widest = array.shape.index(max(array.shape))
    neighbour = spot[:widest] + [(spot[widest] + 1) % array.shape[widest]] + spot[widest + 1:]
    return array.at[tuple(spot)].set(low).at[tuple(neighbour)].set(top_value)


def shard_levels(own_key, shape, cuts, smallest, top_value):
    loudness, own = 1.0, jax.random.fold_in(own_key, 6)
    for dim, blocks in cuts:
        steps = jnp.exp(jax.random.uniform(jax.random.fold_in(own, dim), (blocks,), jnp.float32, smallest / len(cuts), top_value / len(cuts)))
        loudness = loudness * jnp.repeat(steps, shape[dim] // blocks).reshape([-1 if axis == dim else 1 for axis in range(len(shape))])
    return loudness


def gaussian(key, shape, deviation, most, cuts=(), kind=jnp.bfloat16):
    result = deviation * jax.random.normal(key, shape, jnp.float32)
    if cuts:
        result = result * shard_levels(key, shape, cuts, -0.22, 0.18)
    return jnp.clip(result, -most, most).astype(kind)


def setup_inputs(seed: int = 0) -> dict:
    arg_keys = jax.random.split(jax.random.key(seed), 12)
    traces = draw_traces(jax.random.fold_in(arg_keys[11], 71), 0)
    targets = gaussian(arg_keys[1], (TRACES, NS), 12.0, 64.0, ((0, 32),))
    src_local = set_ends(jax.random.randint(arg_keys[2], (TRACES,), 0, SRC_DEV), jax.random.fold_in(arg_keys[2], 1), 0, SRC_DEV - 1).astype(jnp.int32)
    rcv_term = draw_rcv_term(jax.random.fold_in(arg_keys[11], 71), 0)
    cmp_term = draw_cmp_term(jax.random.fold_in(arg_keys[11], 71), 0)
    rcv_home = draw_rcv_home(jax.random.fold_in(arg_keys[11], 71), 0)
    cmp_home = draw_cmp_home(jax.random.fold_in(arg_keys[11], 71), 0)
    counts = draw_counts(jax.random.fold_in(arg_keys[11], 71), 0)
    src_filters = gaussian(arg_keys[8], (NSRC, TAPS), 0.3, 1.75, ((0, 32),), jnp.float32)
    rcv_filters = gaussian(arg_keys[9], (NRCV, TAPS), 0.3, 1.75, ((0, 32),), jnp.float32)
    cmp_filters = gaussian(arg_keys[10], (NCMP, TAPS), 0.3, 1.75, ((0, 32),), jnp.float32)
    return dict(traces=traces, targets=targets, src_local=src_local, rcv_term=rcv_term, cmp_term=cmp_term, rcv_home=rcv_home, cmp_home=cmp_home, counts=counts, src_filters=src_filters, rcv_filters=rcv_filters, cmp_filters=cmp_filters)


def trace_terms(pieces):
    trace_data, target_data, filter_rows, live_rows = pieces
    row_width = NS + TAPS
    signal = trace_data.astype(jnp.float32)
    signal_spectrum = jnp.fft.rfft(signal, n=row_width, axis=1)
    filter_spectrum = jnp.fft.rfft(filter_rows.astype(jnp.float32), n=row_width, axis=1)
    model_trace = jnp.fft.irfft(signal_spectrum * filter_spectrum, n=row_width, axis=1)[:, :NS]
    difference = model_trace - target_data.astype(jnp.float32)
    misfit = jnp.where(live_rows[:, None], difference, jnp.zeros_like(difference)).astype(jnp.bfloat16)
    misfit_spectrum = jnp.fft.rfft(misfit.astype(jnp.float32), n=row_width, axis=1)
    grad_trace = jnp.fft.irfft(misfit_spectrum * jnp.conj(signal_spectrum), n=row_width, axis=1)[:, :TAPS]
    squares = jnp.sum(signal * signal, axis=1)
    power = jnp.where(live_rows, squares, jnp.zeros_like(squares))
    return grad_trace, power


def reference(traces, targets, src_local, rcv_term, cmp_term, rcv_home, cmp_home, counts, src_filters, rcv_filters, cmp_filters):
    slot_index = jnp.arange(TRACES, dtype=jnp.int32)
    device_of = slot_index // TR_DEV
    src_slot = (device_of * SRC_DEV + src_local).astype(jnp.int32)
    rcv_slot = rcv_home[rcv_term].astype(jnp.int32)
    cmp_slot = cmp_home[cmp_term].astype(jnp.int32)
    live_mask = (slot_index % TR_DEV) < counts[device_of]
    mixed_filters = ((src_filters[src_slot] + rcv_filters[rcv_slot]) + cmp_filters[cmp_slot]).astype(jnp.bfloat16)
    grad_trace, power = lax.map(trace_terms, (
        traces.reshape(DEVICES, TR_DEV, NS),
        targets.reshape(DEVICES, TR_DEV, NS),
        mixed_filters.reshape(DEVICES, TR_DEV, TAPS),
        live_mask.reshape(DEVICES, TR_DEV)))
    grad_trace = grad_trace.reshape(TRACES, TAPS)
    power = power.reshape(TRACES)

    def settle(filter_table, slots, term_count):
        grad_sum = jax.ops.segment_sum(grad_trace, slots, num_segments=term_count)
        power_sum = jax.ops.segment_sum(power, slots, num_segments=term_count)
        return filter_table - 0.5 * grad_sum / jnp.maximum(power_sum, 1.0)[:, None]

    return (settle(src_filters, src_slot, NSRC),
            settle(rcv_filters, rcv_slot, NRCV),
            settle(cmp_filters, cmp_slot, NCMP))
```

```python
import functools

import jax
import jax.numpy as jnp
import numpy as np
from jax import lax
from jax.experimental import pallas as pl
from jax.experimental.pallas import tpu as pltpu
from jax.sharding import PartitionSpec as P

STEP = 0.5
BF = jnp.bfloat16
F32 = jnp.float32
AXES = ("shot", "line")
ROWS = 64
VMEM_LIMIT = 48 * 1024 * 1024


def halves(matrix):
    high = matrix.astype(jnp.bfloat16)
    low = (matrix - high.astype(np.float64)).astype(jnp.bfloat16)
    return high, low


def spectral_tables(taps):
    span = 2 * taps
    theta = 2 * np.pi * (np.arange(taps) + 0.5) / span
    angle = np.arange(span)[:, None] * theta[None, :]
    forward = np.concatenate([np.cos(angle), -np.sin(angle)], axis=1)
    inverse = forward.T / taps
    even = 2 * np.cos(angle[:taps])
    even[0] = 1.0
    fwd_high, fwd_low = halves(forward[:taps])
    twice = np.concatenate([fwd_high, fwd_low], axis=0)

    def triple(matrix):
        high, low = halves(matrix)
        return np.concatenate([high, high, low], axis=0)

    return (
        twice,
        triple(inverse[:, :taps] @ even),
        triple(inverse[:, taps:] @ forward[taps:]),
        triple(inverse[:, :taps]),
    )


def mm(left, right):
    return jnp.dot(left, right, preferred_element_type=F32)


def mm_t(left, right):
    return lax.dot_general(left, right, (((0,), (0,)), ((), ())), preferred_element_type=F32)


def split3(value):
    high = value.astype(BF)
    rest = value - high.astype(F32)
    middle = rest.astype(BF)
    low = (rest - middle.astype(F32)).astype(BF)
    return high, middle, low


def exact_mm(onehot, value):
    high, middle, low = split3(value)
    return mm(onehot, high) + mm(onehot, middle) + mm(onehot, low)


def fine_mm(value, table):
    high = value.astype(BF)
    low = (value - high.astype(F32)).astype(BF)
    return mm(jnp.concatenate([high, low, high], axis=1), table)


def iota(shape, dim):
    return lax.broadcasted_iota(jnp.int32, shape, dim)


def pick_mask(condition):
    return jnp.where(condition, 1.0, 0.0).astype(BF)


def row_to_lanes(row):
    return jnp.transpose(jnp.broadcast_to(row, (128, row.shape[1])))


def find_slots(term_row, home, terms_dev, slot_cap):
    count = term_row.shape[1]
    shift = terms_dev.bit_length() - 1
    lane = iota((count, 128), 1)
    term = row_to_lanes(term_row)
    chunks = home.shape[0]
    high_term, low_term = term >> 7, term & 127
    if chunks <= 128:
        onehot = pick_mask(lane[:, :chunks] == high_term[:, :chunks])
    else:
        onehot = jnp.concatenate(
            [pick_mask(lane + base == high_term) for base in range(0, chunks, 128)], axis=1
        )
    ones = jnp.ones((128, 128), BF)
    here = lane == low_term
    high = mm(onehot, (home >> 7).astype(F32).astype(BF))
    low = mm(onehot, (home & 127).astype(F32).astype(BF))
    high = mm(jnp.where(here, high, 0.0).astype(BF), ones)
    low = mm(jnp.where(here, low, 0.0).astype(BF), ones)
    row = high.astype(jnp.int32) * 128 + low.astype(jnp.int32)
    owner = row >> shift
    place = (row & (terms_dev - 1)).astype(F32)
    owner_hot = pick_mask(lane == owner)
    earlier = pick_mask(iota((count, count), 1) < iota((count, count), 0))
    before = mm(earlier, owner_hot)
    rank = mm(jnp.where(lane == owner, before, 0.0).astype(BF), ones).astype(jnp.int32)
    rank_hot = lane == rank
    request = mm_t(owner_hot, jnp.where(rank_hot, place, 0.0).astype(BF))
    return owner_hot, rank_hot, owner * slot_cap + rank, request


def spread_rows(rows, slot_cap):
    device_count = rows.shape[0]
    slots = device_count * slot_cap
    shift = slot_cap.bit_length() - 1
    where = pick_mask((iota((device_count, slots), 1) >> shift) == iota((device_count, slots), 0))
    high, middle, low = split3(rows)
    wide = mm_t(high, where) + mm_t(middle, where) + mm_t(low, where)
    mine = (iota((128, slots), 1) & (slot_cap - 1)) == iota((128, slots), 0)
    return jnp.sum(jnp.where(mine, wide, 0.0), axis=0, keepdims=True)


def spread_cols(rows, slot_cap):
    device_count = rows.shape[0]
    slots = device_count * slot_cap
    shift = slot_cap.bit_length() - 1
    where = pick_mask((iota((slots, device_count), 0) >> shift) == iota((slots, device_count), 1))
    wide = mm(where, rows.astype(BF))
    mine = (iota((slots, 128), 0) & (slot_cap - 1)) == iota((slots, 128), 1)
    return mm(jnp.where(mine, wide, 0.0).astype(BF), jnp.ones((128, 128), BF))


def lookup(request, filters, slot_cap):
    place = spread_cols(request, slot_cap).astype(jnp.int32)
    lane = iota(place.shape, 1)
    onehot = jnp.concatenate(
        [pick_mask(lane + base == place) for base in range(0, filters.shape[0], 128)], axis=1
    )
    return exact_mm(onehot, filters)


def spectra_rows(trace_rows, target_rows, twice, even, spec_x, spec_t):
    taps = twice.shape[0] // 2
    rows, samples = trace_rows.shape
    blocks = samples // taps

    def stacked(value):
        tall = jnp.concatenate([value[:, b * taps : (b + 1) * taps] for b in range(blocks)], axis=0)
        return jnp.concatenate([tall, tall], axis=1)

    spec_x[...] = mm(stacked(trace_rows), twice)
    spec_t[...] = mm(stacked(target_rows), twice)
    sign = 1.0 - 2.0 * (iota((16, taps), 1) & 1).astype(F32)
    out = []
    for start in range(0, rows, 16):
        c0r = c0i = c1r = c1i = p0 = p1r = p1i = jnp.zeros((16, taps), F32)
        xr0 = xi0 = None
        for b in range(blocks):
            here = pl.ds(b * rows + start, 16)
            xr, xi = spec_x[here, :taps], spec_x[here, taps:]
            tr, ti = spec_t[here, :taps], spec_t[here, taps:]
            c0r += xr * tr + xi * ti
            c0i += xr * ti - xi * tr
            p0 += xr * xr + xi * xi
            if b:
                c1r += xr0 * tr + xi0 * ti
                c1i += xr0 * ti - xi0 * tr
                p1r += xr0 * xr + xi0 * xi
                p1i += xr0 * xi - xi0 * xr
            xr0, xi0 = xr, xi
        power = jnp.sum(p0, axis=1, keepdims=True) * (1.0 / taps)
        out.append(
            (
                jnp.concatenate([p0 + sign * p1i, -sign * p1r], axis=1),
                jnp.concatenate([c0r + sign * c1i, c0i - sign * c1r], axis=1),
                jnp.concatenate([xr0, xi0], axis=1),
                jnp.broadcast_to(power, (16, 128)),
            )
        )
    auto, cross, last, power = (jnp.concatenate(parts, axis=0) for parts in zip(*out))
    return fine_mm(auto, even), cross, last, power


def gradients(mixed, q, cross, last, twice, tail, inverse):
    taps = q.shape[1]
    fs = mm(jnp.concatenate([mixed, mixed], axis=1), twice)
    fr, fi = fs[:, :taps], fs[:, taps:]
    xr, xi = last[:, :taps], last[:, taps:]
    over = fine_mm(jnp.concatenate([xr * fr - xi * fi, xr * fi + xi * fr], axis=1), tail)
    yr, yi = over[:, :taps], over[:, taps:]
    gr = q * fr - cross[:, :taps] - (xr * yr + xi * yi)
    gi = q * fi - cross[:, taps:] - (xr * yi - xi * yr)
    return fine_mm(jnp.concatenate([gr, gi], axis=1), inverse)


def slot_hot(slot, slots):
    lane = iota(slot.shape, 1)
    return jnp.concatenate([pick_mask(lane + base == slot) for base in range(0, slots, 128)], axis=1)


def slot_hot_t(slot, slots):
    row = jnp.transpose(slot)[0:1, :]
    return pick_mask(iota((slots, slot.shape[0]), 0) == row)


def settled(filters, place_row, grad_in, power_row):
    terms = filters.shape[0]
    here = iota((terms, place_row.shape[1]), 0) == place_row.astype(jnp.int32)
    sums = exact_mm(pick_mask(here), grad_in)
    energy = jnp.sum(jnp.where(here, power_row, 0.0), axis=1, keepdims=True)
    return filters - STEP * sums / jnp.maximum(energy, 1.0)


def settled_src(filters, src_row, grads, power):
    terms = filters.shape[0]
    here = pick_mask(iota((8, src_row.shape[1]), 0) == src_row)
    sums = exact_mm(here, grads)[:terms]
    energy = exact_mm(here, power)[:terms]
    return filters - STEP * sums / jnp.maximum(energy, 1.0)


def src_rows(src_row, src_filters):
    here = pick_mask(iota((8, src_row.shape[1]), 0) == src_row)
    high, middle, low = split3(
        jnp.concatenate([src_filters, jnp.zeros((8 - src_filters.shape[0], src_filters.shape[1]), F32)], axis=0)
    )
    return mm_t(here, high) + mm_t(here, middle) + mm_t(here, low)


def index_kernel(device_count, slot_cap, terms, rcv_t, cmp_t, rcv_h, cmp_h, slots, ranks, request):
    for table, (term, home) in enumerate(((rcv_t, rcv_h), (cmp_t, cmp_h))):
        owner_hot, rank_hot, slot, req = find_slots(term[...], home[...], terms[table], slot_cap)
        slots[table] = slot
        request[table] = req[:device_count]


def lookup_kernel(slot_cap, request, rcv, cmp, out):
    out[0] = lookup(request[0], rcv[...], slot_cap)
    out[1] = lookup(request[1], cmp[...], slot_cap)


def spectra_kernel(traces, targets, twice, even, q, cross, last, power, spec_x, spec_t):
    q[...], cross[...], last[...], power[...] = spectra_rows(
        traces[...], targets[...], twice[...], even[...], spec_x, spec_t
    )


def post_kernel(
    device_count, slot_cap, counts, src_row, src_filters, slots, fetched, q, cross, last, power,
    twice, tail, inverse, src_out, send, send_power,
):
    total = device_count * slot_cap
    count = q.shape[0]
    mixed = src_rows(src_row[...], src_filters[...])
    for table in range(2):
        mixed = mixed + exact_mm(slot_hot(slots[table], total), fetched[table])
    grads = gradients(mixed.astype(BF), q[...], cross[...], last[...], twice[...], tail[...], inverse[...])
    live = iota((count, 128), 0) < counts[0]
    grads = jnp.where(live, grads, 0.0)
    powers = jnp.where(live, power[...], 0.0)
    src_out[...] = settled_src(src_filters[...], src_row[...], grads, powers)
    for table in range(2):
        slot = slots[table]
        send[table] = exact_mm(slot_hot_t(slot, total), grads)
        shift = slot_cap.bit_length() - 1
        lane = iota((count, 128), 1)
        owner_hot = pick_mask(lane == slot >> shift)
        high, middle, low = split3(jnp.where(lane == (slot & (slot_cap - 1)), powers, 0.0))
        sent = mm_t(owner_hot, high) + mm_t(owner_hot, middle) + mm_t(owner_hot, low)
        send_power[table] = sent[:device_count]


def settle_kernel(slot_cap, request, got, got_power, rcv, cmp, rcv_out, cmp_out):
    for table, (filters, out) in enumerate(((rcv, rcv_out), (cmp, cmp_out))):
        place_row = spread_rows(request[table], slot_cap)
        power_row = spread_rows(got_power[table], slot_cap)
        out[...] = settled(filters[...], place_row, got[table], power_row)


def call(kernel, outs, cost=None, **kwargs):
    return pl.pallas_call(
        kernel,
        out_shape=outs,
        compiler_params=pltpu.CompilerParams(vmem_limit_bytes=VMEM_LIMIT),
        cost_estimate=cost,
        **kwargs,
    )


def exchange(value):
    return lax.all_to_all(value, AXES, split_axis=1, concat_axis=1, tiled=True)


def body(
    traces, targets, src_local, rcv_term, cmp_term, rcv_home, cmp_home, counts,
    src_filters, rcv_filters, cmp_filters,
):
    trace_rows, samples = traces.shape
    taps = src_filters.shape[1]
    device_count = lax.axis_size(AXES)
    slot_cap = max(2, 2 * trace_rows // device_count)
    total = device_count * slot_cap
    blocks = samples // taps
    terms = (rcv_filters.shape[0], cmp_filters.shape[0])
    twice, even, tail, inverse = (jnp.asarray(table) for table in spectral_tables(taps))
    shape = jax.ShapeDtypeStruct
    src_row = src_local.reshape(1, -1)

    slots, request = call(
        lambda a, b, c, d, s, r: index_kernel(device_count, slot_cap, terms, a, b, c, d, s, None, r),
        (shape((2, trace_rows, 128), jnp.int32), shape((2, device_count, 128), F32)),
    )(
        rcv_term.reshape(1, -1), cmp_term.reshape(1, -1),
        rcv_home.reshape(-1, 128), cmp_home.reshape(-1, 128),
    )
    received = exchange(request)
    values = call(
        functools.partial(lookup_kernel, slot_cap), shape((2, total, taps), F32)
    )(received, rcv_filters, cmp_filters)
    fetched = exchange(values.reshape(2, device_count, slot_cap, taps)).reshape(2, total, taps)

    whole = lambda i: (0, 0)
    block = lambda width: pl.BlockSpec((ROWS, width), lambda i: (i, 0))
    q, cross, last, power = call(
        spectra_kernel,
        tuple(shape((trace_rows, width), F32) for width in (taps, 2 * taps, 2 * taps, 128)),
        cost=pl.CostEstimate(flops=4 * trace_rows * samples * 4 * taps, bytes_accessed=6 * 2**20, transcendentals=0),
        grid=(trace_rows // ROWS,),
        in_specs=[block(samples), block(samples), pl.BlockSpec(twice.shape, whole), pl.BlockSpec(even.shape, whole)],
        out_specs=tuple(block(width) for width in (taps, 2 * taps, 2 * taps, 128)),
        scratch_shapes=[pltpu.VMEM((ROWS * blocks, 2 * taps), F32)] * 2,
    )(traces, targets, twice, even)

    smem = pl.BlockSpec(memory_space=pltpu.SMEM)
    vmem = pl.BlockSpec(memory_space=pltpu.VMEM)
    src_out, send, send_power = call(
        functools.partial(post_kernel, device_count, slot_cap),
        (
            shape(src_filters.shape, F32),
            shape((2, total, taps), F32),
            shape((2, device_count, 128), F32),
        ),
        in_specs=[smem] + [vmem] * 11,
    )(counts, src_row, src_filters, slots, fetched, q, cross, last, power, twice, tail, inverse)
    got = exchange(send.reshape(2, device_count, slot_cap, taps)).reshape(2, total, taps)
    got_power = exchange(send_power)
    rcv_out, cmp_out = call(
        functools.partial(settle_kernel, slot_cap),
        (shape(rcv_filters.shape, F32), shape(cmp_filters.shape, F32)),
    )(received, got, got_power, rcv_filters, cmp_filters)
    return src_out, rcv_out, cmp_out


def solution(mesh):
    rows, flat = P(AXES, None), P(AXES)
    return jax.shard_map(
        body,
        mesh=mesh,
        in_specs=(rows, rows, flat, flat, flat, P(), P(), flat, rows, rows, rows),
        out_specs=(rows, rows, rows),
        check_vma=False,
    )
```

```python
import functools

import jax
import jax.numpy as jnp
import numpy as np
from jax import lax
from jax.experimental import pallas as pl
from jax.experimental.pallas import tpu as pltpu
from jax.sharding import PartitionSpec as P

STEP = 0.5
BF = jnp.bfloat16
F32 = jnp.float32
AXES = ("shot", "line")
ROWS = 64
Z = 4
VMEM_LIMIT = 48 * 1024 * 1024


def halves(matrix):
    high = matrix.astype(jnp.bfloat16)
    low = (matrix - high.astype(np.float64)).astype(jnp.bfloat16)
    return high, low


def spectral_tables(taps):
    span = 2 * taps
    theta = 2 * np.pi * (np.arange(taps) + 0.5) / span
    angle = np.arange(span)[:, None] * theta[None, :]
    forward = np.concatenate([np.cos(angle), -np.sin(angle)], axis=1)
    inverse = forward.T / taps
    even = 2 * np.cos(angle[:taps])
    even[0] = 1.0
    fwd_high, fwd_low = halves(forward[:taps])
    twice = np.concatenate([fwd_high, fwd_low], axis=0)

    def triple(matrix):
        high, low = halves(matrix)
        return np.concatenate([high, high, low], axis=0)

    return (
        twice,
        triple(inverse[:, :taps] @ even),
        triple(inverse[:, taps:] @ forward[taps:]),
        triple(inverse[:, :taps]),
    )


def mm(left, right):
    return jnp.dot(left, right, preferred_element_type=F32)


def mm_t(left, right):
    return lax.dot_general(left, right, (((0,), (0,)), ((), ())), preferred_element_type=F32)


def split3(value):
    high = value.astype(BF)
    rest = value - high.astype(F32)
    middle = rest.astype(BF)
    low = (rest - middle.astype(F32)).astype(BF)
    return high, middle, low


def exact_mm(onehot, value):
    high, middle, low = split3(value)
    return mm(onehot, high) + mm(onehot, middle) + mm(onehot, low)


def fine_mm(value, table):
    high = value.astype(BF)
    low = (value - high.astype(F32)).astype(BF)
    return mm(jnp.concatenate([high, low, high], axis=1), table)


def iota(shape, dim):
    return lax.broadcasted_iota(jnp.int32, shape, dim)


def pick_mask(condition):
    return jnp.where(condition, 1.0, 0.0).astype(BF)


def row_to_lanes(row):
    return jnp.transpose(jnp.broadcast_to(row, (128, row.shape[1])))


def find_slots(term_row, home, terms_dev):
    count = term_row.shape[1]
    shift = terms_dev.bit_length() - 1
    lane = iota((count, 128), 1)
    term = row_to_lanes(term_row)
    chunks = home.shape[0]
    high_term, low_term = term >> 7, term & 127
    if chunks <= 128:
        onehot = pick_mask(lane[:, :chunks] == high_term[:, :chunks])
    else:
        onehot = jnp.concatenate(
            [pick_mask(lane + base == high_term) for base in range(0, chunks, 128)], axis=1
        )
    ones = jnp.ones((128, 128), BF)
    here = lane == low_term
    high = mm(onehot, (home >> 7).astype(F32).astype(BF))
    low = mm(onehot, (home & 127).astype(F32).astype(BF))
    high = mm(jnp.where(here, high, 0.0).astype(BF), ones)
    low = mm(jnp.where(here, low, 0.0).astype(BF), ones)
    row = high.astype(jnp.int32) * 128 + low.astype(jnp.int32)
    owner = row >> shift
    place = (row & (terms_dev - 1)).astype(F32)
    earlier = pick_mask(iota((count, count), 1) < iota((count, count), 0))
    before = mm(earlier, pick_mask(lane == owner))
    rank = mm(jnp.where(lane == owner, before, 0.0).astype(BF), ones).astype(jnp.int32)
    return owner, rank, place


def as_row(lanes):
    return jnp.transpose(lanes)[0:1, :]


def both_hot(slots, base, width):
    lane = iota(slots[0].shape, 1)
    parts = []
    for start in range(0, width, 128):
        here = lane + (base + start)
        parts.append(pick_mask((here == slots[0]) | (here == slots[1])))
    return jnp.concatenate(parts, axis=1)


def spectra_rows(trace_rows, target_rows, twice, even, spec_x, spec_t):
    taps = twice.shape[0] // 2
    rows, samples = trace_rows.shape
    blocks = samples // taps

    def stacked(value):
        tall = jnp.concatenate([value[:, b * taps : (b + 1) * taps] for b in range(blocks)], axis=0)
        return jnp.concatenate([tall, tall], axis=1)

    spec_x[...] = mm(stacked(trace_rows), twice)
    spec_t[...] = mm(stacked(target_rows), twice)
    sign = 1.0 - 2.0 * (iota((16, taps), 1) & 1).astype(F32)
    out = []
    for start in range(0, rows, 16):
        c0r = c0i = c1r = c1i = p0 = p1r = p1i = jnp.zeros((16, taps), F32)
        xr0 = xi0 = None
        for b in range(blocks):
            here = pl.ds(b * rows + start, 16)
            xr, xi = spec_x[here, :taps], spec_x[here, taps:]
            tr, ti = spec_t[here, :taps], spec_t[here, taps:]
            c0r += xr * tr + xi * ti
            c0i += xr * ti - xi * tr
            p0 += xr * xr + xi * xi
            if b:
                c1r += xr0 * tr + xi0 * ti
                c1i += xr0 * ti - xi0 * tr
                p1r += xr0 * xr + xi0 * xi
                p1i += xr0 * xi - xi0 * xr
            xr0, xi0 = xr, xi
        power = jnp.sum(p0, axis=1, keepdims=True) * (1.0 / taps)
        out.append(
            (
                jnp.concatenate([p0 + sign * p1i, -sign * p1r], axis=1),
                jnp.concatenate([c0r + sign * c1i, c0i - sign * c1r], axis=1),
                jnp.concatenate([xr0, xi0], axis=1),
                jnp.broadcast_to(power, (16, 128)),
            )
        )
    auto, cross, last, power = (jnp.concatenate(parts, axis=0) for parts in zip(*out))
    return fine_mm(auto, even), cross, last, power


def gradients(mixed, q, cross, last, twice, tail, inverse):
    taps = q.shape[1]
    fs = mm(jnp.concatenate([mixed, mixed], axis=1), twice)
    fr, fi = fs[:, :taps], fs[:, taps:]
    xr, xi = last[:, :taps], last[:, taps:]
    over = fine_mm(jnp.concatenate([xr * fr - xi * fi, xr * fi + xi * fr], axis=1), tail)
    yr, yi = over[:, :taps], over[:, taps:]
    gr = q * fr - cross[:, :taps] - (xr * yr + xi * yi)
    gi = q * fi - cross[:, taps:] - (xr * yi - xi * yr)
    return fine_mm(jnp.concatenate([gr, gi], axis=1), inverse)


def settled_src(filters, src_row, grads, power):
    terms = filters.shape[0]
    here = pick_mask(iota((8, src_row.shape[1]), 0) == src_row)
    sums = exact_mm(here, grads)[:terms]
    energy = exact_mm(here, power)[:terms]
    return filters - STEP * sums / jnp.maximum(energy, 1.0)


def src_rows(src_row, src_filters):
    here = pick_mask(iota((8, src_row.shape[1]), 0) == src_row)
    high, middle, low = split3(
        jnp.concatenate([src_filters, jnp.zeros((8 - src_filters.shape[0], src_filters.shape[1]), F32)], axis=0)
    )
    return mm_t(here, high) + mm_t(here, middle) + mm_t(here, low)


def fused_kernel(
    sizes, counts, traces, targets, src_row, rcv_row, cmp_row, rcv_home, cmp_home,
    src_f, rcv_f, cmp_f, twice, even, tail, inverse,
    src_out, rcv_out, cmp_out,
    v_traces, v_targets, v_src_row, v_rcv_row, v_cmp_row, v_rcv_home, v_cmp_home,
    v_src_f, v_twice, v_even, v_tail, v_inverse,
    table, req_send, req_recv, vals, fetched, hot, grad_send, grad_recv, part, inbox,
    q, cross, last, power, spec_x, spec_t,
    local_sem, req_ss, req_rs, tab_ss, tab_rs, val_ss, val_rs, grad_ss, grad_rs, part_ss, part_rs,
):
    lines, plane, slot_cap, terms = sizes
    rcv_terms, cmp_terms = terms
    rows_all = rcv_terms + cmp_terms
    pair = 2 * slot_cap
    width = plane * pair
    count = v_traces.shape[0]
    me = lax.axis_index("shot") * lines + lax.axis_index("line")
    z, p = me // plane, me % plane

    def device(index):
        return (index // lines, index % lines)

    def peer(offset):
        return (p + offset) % plane

    def remote(source, target, send, recv, index):
        return pltpu.make_async_remote_copy(
            src_ref=source, dst_ref=target, send_sem=send, recv_sem=recv,
            device_id=device(index), device_id_type=pl.DeviceIdType.MESH,
        )

    small = [
        (rcv_row, v_rcv_row), (cmp_row, v_cmp_row), (rcv_home, v_rcv_home), (cmp_home, v_cmp_home),
        (rcv_f, table.at[z, pl.ds(0, rcv_terms)]), (cmp_f, table.at[z, pl.ds(rcv_terms, cmp_terms)]),
        (src_row, v_src_row), (src_f, v_src_f), (twice, v_twice), (even, v_even),
        (tail, v_tail), (inverse, v_inverse), (traces, v_traces), (targets, v_targets),
    ]
    copies = [
        pltpu.make_async_copy(source, target, local_sem.at[i]) for i, (source, target) in enumerate(small)
    ]
    for copy in copies:
        copy.start()
    barrier = pltpu.get_barrier_semaphore()

    def greet(index):
        pl.semaphore_signal(barrier, inc=1, device_id=device(index), device_id_type=pl.DeviceIdType.MESH)

    for offset in range(1, plane):
        greet(z * plane + peer(offset))
    for distance in range(1, Z):
        greet((z + distance) % Z * plane + p)
    pl.semaphore_wait(barrier, plane - 1 + Z - 1)

    def table_copy(way, distance):
        chunk = z - distance if way == 0 else z + distance
        target = me + plane if way == 0 else me - plane
        return remote(
            table.at[chunk], table.at[chunk], tab_ss.at[way, distance], tab_rs.at[way, distance + 1], target
        )

    def table_wait(way, distance):
        chunk = z - distance if way == 0 else z + distance
        remote(
            table.at[chunk], table.at[chunk], tab_ss.at[way, distance], tab_rs.at[way, distance], me
        ).wait_recv()

    def arrives(way, distance):
        return z >= distance if way == 0 else z <= Z - 1 - distance

    def goes_on(way, distance):
        return ((z >= distance) & (z < Z - 1)) if way == 0 else ((z <= Z - 1 - distance) & (z > 0))

    copies[4].wait()
    copies[5].wait()
    for way in range(2):
        pl.when(goes_on(way, 0))(lambda way=way: table_copy(way, 0).start())
    for i in range(4):
        copies[i].wait()

    found = [
        find_slots(v_rcv_row[...], v_rcv_home[...], rcv_terms),
        find_slots(v_cmp_row[...], v_cmp_home[...], cmp_terms),
    ]
    lane = iota((count, 128), 1)
    req_rows = 2 * Z * plane
    req_iota = iota((req_rows, count), 0)
    wanted = ((req_iota >> 1) & (Z - 1)) * plane + req_iota // (2 * Z)
    slots, slot_rows, owner_rows, rank_hots = [], [], [], []
    request = jnp.zeros((req_rows, 128), F32)
    for kind, (owner, rank, place) in enumerate(found):
        owner_row = as_row(owner)
        slot = owner * pair + (kind * slot_cap + rank)
        rank_hot = lane == rank
        lhs = pick_mask((wanted == owner_row) & ((req_iota & 1) == kind))
        request = request + mm(lhs, jnp.where(rank_hot, place, 0.0).astype(BF))
        slots.append(slot)
        slot_rows.append(as_row(slot))
        owner_rows.append(owner_row)
        rank_hots.append(rank_hot)
    req_send[...] = request.reshape(plane, 2 * Z, 128)
    req_copies = [
        remote(
            req_send.at[peer(offset)], req_recv.at[p], req_ss.at[offset], req_rs.at[p],
            z * plane + peer(offset),
        )
        for offset in range(1, plane)
    ]
    for copy in req_copies:
        copy.start()
    req_recv[pl.ds(p, 1)] = req_send[pl.ds(p, 1)]

    for i in range(6, 14):
        copies[i].wait()

    def spectra(start, stop):
        @pl.loop(start, stop)
        def _(turn):
            here = pl.ds(pl.multiple_of(turn * ROWS, ROWS), ROWS)
            q[here, :], cross[here, :], last[here, :], power[here, :] = spectra_rows(
                v_traces[here, :], v_targets[here, :], v_twice[...], v_even[...], spec_x, spec_t
            )

    turns = count // ROWS
    spectra(0, turns // 4)

    for offset in range(1, plane):
        source = peer(offset)
        remote(
            req_send.at[source], req_recv.at[source], req_ss.at[offset], req_rs.at[source], me
        ).wait_recv()

    cap_bits = slot_cap.bit_length() - 1

    def value_copy(chunk, offset):
        return remote(
            vals.at[chunk, peer(offset)], fetched.at[chunk, p], val_ss.at[chunk, offset],
            val_rs.at[chunk, p], z * plane + peer(offset),
        )

    def serve(chunk):
        request_rows = req_recv[...].reshape(plane * 2 * Z, 128).astype(BF)
        row = iota((width, plane * 2 * Z), 0)
        col = iota((width, plane * 2 * Z), 1)
        kind = (row >> cap_bits) & 1
        expand = pick_mask(col == (row >> (cap_bits + 1)) * (2 * Z) + 2 * chunk + kind)
        wide = mm(expand, request_rows)
        row = iota((width, 128), 0)
        mine = (row & (slot_cap - 1)) == iota((width, 128), 1)
        place = mm(jnp.where(mine, wide, 0.0).astype(BF), jnp.ones((128, 128), BF)).astype(jnp.int32)
        place = place + ((row >> cap_bits) & 1) * rcv_terms
        onehot = jnp.concatenate(
            [pick_mask(iota((width, 128), 1) + base == place) for base in range(0, rows_all, 128)], axis=1
        )
        hot[chunk] = onehot
        vals[chunk] = exact_mm(onehot, table[chunk]).reshape(plane, pair, 128)
        for offset in range(1, plane):
            value_copy(chunk, offset).start()
        fetched[chunk, pl.ds(p, 1)] = vals[chunk, pl.ds(p, 1)]

    serve(z)
    marks = [turns // 4, turns // 2, 3 * turns // 4, turns]
    for distance in range(1, Z):
        for way in range(2):
            pl.when(arrives(way, distance))(lambda way=way: table_wait(way, distance))
            if distance < Z - 1:
                pl.when(goes_on(way, distance))(lambda way=way: table_copy(way, distance).start())
        for way in range(2):
            chunk = z - distance if way == 0 else z + distance
            pl.when(arrives(way, distance))(lambda chunk=chunk: serve(chunk))
        spectra(marks[distance - 1], marks[distance])

    mixed = src_rows(v_src_row[...], v_src_f[...])
    for chunk in range(Z):
        for offset in range(1, plane):
            source = peer(offset)
            remote(
                vals.at[chunk, source], fetched.at[chunk, source], val_ss.at[chunk, offset],
                val_rs.at[chunk, source], me,
            ).wait_recv()
        mixed = mixed + exact_mm(
            both_hot(slots, chunk * width, width), fetched[chunk].reshape(width, 128)
        )
    grads = gradients(
        mixed.astype(BF), q[...], cross[...], last[...], v_twice[...], v_tail[...], v_inverse[...]
    )
    live = iota((count, 128), 0) < counts[0]
    grads = jnp.where(live, grads, 0.0)
    powers = jnp.where(live, power[...], 0.0)
    grad_parts = split3(grads)
    power_parts = [split3(jnp.where(rank_hot, powers, 0.0)) for rank_hot in rank_hots]

    order = (3 * (1 - z // 2), (2 + 3 * z) % 5, 1 + z % 2, z)

    def grad_copy(chunk, offset):
        return remote(
            grad_send.at[chunk, peer(offset)], grad_recv.at[chunk, p], grad_ss.at[chunk, offset],
            grad_rs.at[chunk, p], z * plane + peer(offset),
        )

    for chunk in order:
        row = iota((width, count), 0) + chunk * width
        onehot = pick_mask((row == slot_rows[0]) | (row == slot_rows[1]))
        sent = mm(onehot, grad_parts[0]) + mm(onehot, grad_parts[1]) + mm(onehot, grad_parts[2])
        grad_send[chunk, :, pl.ds(0, pair), :] = sent.reshape(plane, pair, 128)
        row = iota((plane * 8, count), 0)
        energy = jnp.zeros((plane * 8, 128), F32)
        for kind in range(2):
            onehot = pick_mask(((row >> 3) + chunk * plane == owner_rows[kind]) & ((row & 7) == kind))
            for piece in power_parts[kind]:
                energy = energy + mm(onehot, piece)
        grad_send[chunk, :, pl.ds(pair, 8), :] = energy.reshape(plane, 8, 128)
        for offset in range(1, plane):
            grad_copy(chunk, offset).start()
        grad_recv[chunk, pl.ds(p, 1)] = grad_send[chunk, pl.ds(p, 1)]
    src_out[...] = settled_src(v_src_f[...], v_src_row[...], grads, powers)

    def part_copy(chunk, way):
        target = me + plane if way == 0 else me - plane
        return remote(
            part.at[chunk], inbox.at[way, chunk], part_ss.at[chunk], part_rs.at[way, chunk], target
        )

    def add_inbox(chunk, way):
        remote(
            part.at[chunk], inbox.at[way, chunk], part_ss.at[chunk], part_rs.at[way, chunk], me
        ).wait_recv()
        part[chunk] = part[chunk] + inbox[way, chunk]

    for step, chunk in enumerate(order):
        for offset in range(1, plane):
            source = peer(offset)
            remote(
                grad_send.at[chunk, source], grad_recv.at[chunk, source], grad_ss.at[chunk, offset],
                grad_rs.at[chunk, source], me,
            ).wait_recv()
        onehot = hot[chunk]
        got = split3(grad_recv[chunk, :, pl.ds(0, pair), :].reshape(width, 128))
        part[chunk, pl.ds(0, rows_all)] = mm_t(onehot, got[0]) + mm_t(onehot, got[1]) + mm_t(onehot, got[2])
        energy = grad_recv[chunk, :, pl.ds(pair, 8), :].reshape(plane * 8, 128)
        row, col = iota((plane * 8, width), 0), iota((plane * 8, width), 1)
        spread = pick_mask(
            ((row >> 3) == (col >> (cap_bits + 1))) & ((row & 7) == ((col >> cap_bits) & 1))
        )
        wide = sum(mm_t(piece, spread) for piece in split3(energy))
        mine = (iota((128, width), 1) & (slot_cap - 1)) == iota((128, width), 0)
        energy = jnp.sum(jnp.where(mine, wide, 0.0), axis=0, keepdims=True)
        energy = sum(mm(piece, onehot) for piece in split3(jnp.broadcast_to(energy, (8, width))))
        lines8 = iota((8, 128), 0)
        packed = jnp.zeros((8, 128), F32)
        for i in range(rows_all // 128):
            packed = packed + jnp.where(lines8 == i, energy[:, i * 128 : (i + 1) * 128], 0.0)
        part[chunk, pl.ds(rows_all, 8)] = packed
        pl.when((chunk >= z) & (z > 0))(lambda chunk=chunk: add_inbox(chunk, 0))
        pl.when((chunk <= z) & (z < Z - 1))(lambda chunk=chunk: add_inbox(chunk, 1))
        if step < Z - 1:
            pl.when(chunk > z)(lambda chunk=chunk: part_copy(chunk, 0).start())
            pl.when(chunk < z)(lambda chunk=chunk: part_copy(chunk, 1).start())

    packed = part[z, pl.ds(rows_all, 8)]
    for i in range(rows_all // 128):
        energy = jnp.transpose(jnp.broadcast_to(packed[i : i + 1, :], (128, 128)))
        here = pl.ds(i * 128, 128)
        updated = table[z, here] - STEP * part[z, here] / jnp.maximum(energy, 1.0)
        if i * 128 < rcv_terms:
            rcv_out[here, :] = updated
        else:
            cmp_out[pl.ds(i * 128 - rcv_terms, 128), :] = updated

    for copy in req_copies:
        copy.wait_send()
    for distance in range(Z - 1):
        for way in range(2):
            pl.when(goes_on(way, distance))(lambda way=way: table_copy(way, distance).wait_send())
    for chunk in range(Z):
        for offset in range(1, plane):
            value_copy(chunk, offset).wait_send()
            grad_copy(chunk, offset).wait_send()
        pl.when(z != chunk)(lambda chunk=chunk: part_copy(chunk, 0).wait_send())


def body(
    traces, targets, src_local, rcv_term, cmp_term, rcv_home, cmp_home, counts,
    src_filters, rcv_filters, cmp_filters,
):
    trace_rows, samples = traces.shape
    taps = src_filters.shape[1]
    device_count = lax.axis_size(AXES)
    lines = lax.axis_size("line")
    slot_cap = max(2, 2 * trace_rows // device_count)
    plane = device_count // Z
    pair = 2 * slot_cap
    blocks = samples // taps
    terms = (rcv_filters.shape[0], cmp_filters.shape[0])
    rows_all = sum(terms)
    tables = tuple(jnp.asarray(table) for table in spectral_tables(taps))
    shape = jax.ShapeDtypeStruct
    vmem, sem = pltpu.VMEM, pltpu.SemaphoreType.DMA
    operands = (
        traces, targets, src_local.reshape(1, -1), rcv_term.reshape(1, -1), cmp_term.reshape(1, -1),
        rcv_home.reshape(-1, 128), cmp_home.reshape(-1, 128),
        src_filters, rcv_filters, cmp_filters, *tables,
    )
    held = [vmem(x.shape, x.dtype) for x in operands[:8] + tables]
    return pl.pallas_call(
        functools.partial(fused_kernel, (lines, plane, slot_cap, terms)),
        out_shape=tuple(shape(x.shape, F32) for x in (src_filters, rcv_filters, cmp_filters)),
        in_specs=[pl.BlockSpec(memory_space=pltpu.SMEM)]
        + [pl.BlockSpec(memory_space=pl.ANY)] * len(operands),
        out_specs=(pl.BlockSpec(memory_space=pltpu.VMEM),) * 3,
        scratch_shapes=held
        + [
            vmem((Z, rows_all, 128), F32),
            vmem((plane, 2 * Z, 128), F32),
            vmem((plane, 2 * Z, 128), F32),
            vmem((Z, plane, pair, 128), F32),
            vmem((Z, plane, pair, 128), F32),
            vmem((Z, plane * pair, rows_all), BF),
            vmem((Z, plane, pair + 8, 128), F32),
            vmem((Z, plane, pair + 8, 128), F32),
            vmem((Z, rows_all + 8, 128), F32),
            vmem((2, Z, rows_all + 8, 128), F32),
            vmem((trace_rows, taps), F32),
            vmem((trace_rows, 2 * taps), F32),
            vmem((trace_rows, 2 * taps), F32),
            vmem((trace_rows, 128), F32),
            vmem((ROWS * blocks, 2 * taps), F32),
            vmem((ROWS * blocks, 2 * taps), F32),
            sem((14,)),
            sem((plane,)), sem((plane,)),
            sem((2, Z)), sem((2, Z + 1)),
            sem((Z, plane)), sem((Z, plane)),
            sem((Z, plane)), sem((Z, plane)),
            sem((Z,)), sem((2, Z)),
        ],
        compiler_params=pltpu.CompilerParams(
            vmem_limit_bytes=VMEM_LIMIT, collective_id=0, has_side_effects=True
        ),
        cost_estimate=pl.CostEstimate(
            flops=16 * trace_rows * samples * taps, bytes_accessed=6 * 2**20, transcendentals=0
        ),
    )(counts, *operands)


def solution(mesh):
    rows, flat = P(AXES, None), P(AXES)
    return jax.shard_map(
        body,
        mesh=mesh,
        in_specs=(rows, rows, flat, flat, flat, P(), P(), flat, rows, rows, rows),
        out_specs=(rows, rows, rows),
        check_vma=False,
    )
```

```python
import functools

import jax
import jax.numpy as jnp
import numpy as np
from jax import lax
from jax.experimental import pallas as pl
from jax.experimental.pallas import tpu as pltpu
from jax.sharding import PartitionSpec as P

STEP = 0.5
BF = jnp.bfloat16
F32 = jnp.float32
AXES = ("shot", "line")
ROWS = 64
Z = 4
VMEM_LIMIT = 60 * 1024 * 1024


def halves(matrix):
    high = matrix.astype(jnp.bfloat16)
    low = (matrix - high.astype(np.float64)).astype(jnp.bfloat16)
    return high, low


def spectral_tables(taps):
    span = 2 * taps
    theta = 2 * np.pi * (np.arange(taps) + 0.5) / span
    angle = np.arange(span)[:, None] * theta[None, :]
    forward = np.concatenate([np.cos(angle), -np.sin(angle)], axis=1)
    inverse = forward.T / taps
    even = 2 * np.cos(angle[:taps])
    even[0] = 1.0
    fwd_high, fwd_low = halves(forward[:taps])
    twice = np.concatenate([fwd_high, fwd_low], axis=0)

    def triple(matrix):
        high, low = halves(matrix)
        return np.concatenate([high, high, low], axis=0)

    def tall(matrix):
        return np.concatenate([matrix[:, :128], matrix[:, 128:]], axis=0)

    return (
        tall(twice),
        triple(inverse[:, :taps] @ even),
        tall(triple(inverse[:, taps:] @ forward[taps:])),
        triple(inverse[:, :taps]),
    )


def mm(left, right):
    return jnp.dot(left, right, preferred_element_type=F32)


def mm_t(left, right):
    return lax.dot_general(left, right, (((0,), (0,)), ((), ())), preferred_element_type=F32)


def split2(value):
    high = value.astype(BF)
    return jnp.concatenate([high, (value - high.astype(F32)).astype(BF)], axis=1)


def folded(wide):
    half = wide.shape[1] // 2
    return wide[:, :half] + wide[:, half:]


def pick_mm(onehot, parts):
    return folded(mm(onehot, parts))


def fine_mm(value, table):
    high = value.astype(BF)
    low = (value - high.astype(F32)).astype(BF)
    return mm(jnp.concatenate([high, low, high], axis=1), table)


def iota(shape, dim):
    return lax.broadcasted_iota(jnp.int32, shape, dim)


def pick_mask(condition):
    return jnp.where(condition, 1.0, 0.0).astype(BF)


def row_to_lanes(row):
    return jnp.transpose(jnp.broadcast_to(row, (128, row.shape[1])))


def find_slots(term_row, home, terms_dev):
    count = term_row.shape[1]
    shift = terms_dev.bit_length() - 1
    lane = iota((count, 128), 1)
    term = row_to_lanes(term_row)
    chunks = home.shape[0]
    high_term, low_term = term >> 7, term & 127
    if chunks <= 128:
        onehot = pick_mask(lane[:, :chunks] == high_term[:, :chunks])
    else:
        onehot = jnp.concatenate(
            [pick_mask(lane + base == high_term) for base in range(0, chunks, 128)], axis=1
        )
    ones = jnp.ones((128, 128), BF)
    here = lane == low_term
    high = mm(onehot, (home >> 7).astype(F32).astype(BF))
    low = mm(onehot, (home & 127).astype(F32).astype(BF))
    high = mm(jnp.where(here, high, 0.0).astype(BF), ones)
    low = mm(jnp.where(here, low, 0.0).astype(BF), ones)
    row = high.astype(jnp.int32) * 128 + low.astype(jnp.int32)
    owner = row >> shift
    place = (row & (terms_dev - 1)).astype(F32)
    earlier = pick_mask(iota((count, count), 1) < iota((count, count), 0))
    before = mm(earlier, pick_mask(lane == owner))
    rank = mm(jnp.where(lane == owner, before, 0.0).astype(BF), ones).astype(jnp.int32)
    return owner, rank, place


def as_row(lanes):
    return jnp.transpose(lanes)[0:1, :]


def both_hot(slots, base, width):
    lane = iota(slots[0].shape, 1)
    parts = []
    for start in range(0, width, 128):
        here = lane + (base + start)
        parts.append(pick_mask((here == slots[0]) | (here == slots[1])))
    return jnp.concatenate(parts, axis=1)


def spectra_rows(trace_rows, target_rows, twice, even, spec_x, spec_t):
    taps = twice.shape[0] // 2
    rows, samples = trace_rows.shape
    blocks = samples // taps

    def stacked(value):
        tall = jnp.concatenate([value[:, b * taps : (b + 1) * taps] for b in range(blocks)], axis=0)
        return jnp.concatenate([tall, tall], axis=1)

    spec_x[...] = mm(stacked(trace_rows), twice)
    spec_t[...] = mm(stacked(target_rows), twice)
    sign = 1.0 - 2.0 * (iota((16, taps), 1) & 1).astype(F32)
    out = []
    for start in range(0, rows, 16):
        c0r = c0i = c1r = c1i = p0 = p1r = p1i = jnp.zeros((16, taps), F32)
        xr0 = xi0 = None
        for b in range(blocks):
            here = pl.ds(b * rows + start, 16)
            xr, xi = spec_x[here, :taps], spec_x[here, taps:]
            tr, ti = spec_t[here, :taps], spec_t[here, taps:]
            c0r += xr * tr + xi * ti
            c0i += xr * ti - xi * tr
            p0 += xr * xr + xi * xi
            if b:
                c1r += xr0 * tr + xi0 * ti
                c1i += xr0 * ti - xi0 * tr
                p1r += xr0 * xr + xi0 * xi
                p1i += xr0 * xi - xi0 * xr
            xr0, xi0 = xr, xi
        power = jnp.sum(p0, axis=1, keepdims=True) * (1.0 / taps)
        out.append(
            (
                jnp.concatenate([p0 + sign * p1i, -sign * p1r], axis=1),
                jnp.concatenate([c0r + sign * c1i, c0i - sign * c1r], axis=1),
                jnp.concatenate([xr0, xi0], axis=1),
                jnp.broadcast_to(power, (16, 128)),
            )
        )
    auto, cross, last, power = (jnp.concatenate(parts, axis=0) for parts in zip(*out))
    return fine_mm(auto, even), cross, last, power


def gradients(mixed, q, cross, last, twice, tail, inverse):
    taps = q.shape[1]
    fs = mm(jnp.concatenate([mixed, mixed], axis=1), twice)
    fr, fi = fs[:, :taps], fs[:, taps:]
    xr, xi = last[:, :taps], last[:, taps:]
    over = fine_mm(jnp.concatenate([xr * fr - xi * fi, xr * fi + xi * fr], axis=1), tail)
    yr, yi = over[:, :taps], over[:, taps:]
    gr = q * fr - cross[:, :taps] - (xr * yr + xi * yi)
    gi = q * fi - cross[:, taps:] - (xr * yi - xi * yr)
    return fine_mm(jnp.concatenate([gr, gi], axis=1), inverse)


def settled_src(filters, here, grads, energy):
    terms = filters.shape[0]
    sums = pick_mm(here, split2(grads))[:terms]
    return filters - STEP * sums / jnp.maximum(energy[:terms], 1.0)


def src_rows(here, src_filters):
    missing = jnp.zeros((8 - src_filters.shape[0], src_filters.shape[1]), F32)
    return folded(mm_t(here, split2(jnp.concatenate([src_filters, missing], axis=0))))


def fused_kernel(
    sizes, counts, traces, targets, src_row, rcv_row, cmp_row, rcv_home, cmp_home,
    src_f, rcv_f, cmp_f, twice, even, tail, inverse,
    src_out, rcv_out, cmp_out,
    v_traces, v_targets, v_src_row, v_rcv_row, v_cmp_row, v_rcv_home, v_cmp_home,
    v_src_f, v_twice, v_even, v_tail, v_inverse,
    table, req_send, req_recv, vals, fetched, hot, grad_send, grad_recv, part, inbox,
    mixed, slot_hot, slot_hot_t, q, cross, last, power, spec_x, spec_t,
    local_sem, req_ss, req_rs, tab_ss, tab_rs, val_ss, val_rs, grad_ss, grad_rs, part_ss, part_rs,
):
    lines, plane, slot_cap, terms = sizes
    rcv_terms, cmp_terms = terms
    rows_all = rcv_terms + cmp_terms
    pair = 2 * slot_cap
    width = plane * pair
    count = v_traces.shape[0]
    me = lax.axis_index("shot") * lines + lax.axis_index("line")
    z, p = me // plane, me % plane

    def device(index):
        return (index // lines, index % lines)

    def peer(offset):
        return (p + offset) % plane

    def remote(source, target, send, recv, index):
        return pltpu.make_async_remote_copy(
            src_ref=source, dst_ref=target, send_sem=send, recv_sem=recv,
            device_id=device(index), device_id_type=pl.DeviceIdType.MESH,
        )

    small = [
        (rcv_row, v_rcv_row), (cmp_row, v_cmp_row), (rcv_home, v_rcv_home), (cmp_home, v_cmp_home),
        (rcv_f, table.at[z, pl.ds(0, rcv_terms)]), (cmp_f, table.at[z, pl.ds(rcv_terms, cmp_terms)]),
        (src_row, v_src_row), (src_f, v_src_f), (even, v_even), (inverse, v_inverse),
        (traces, v_traces), (targets, v_targets),
    ]
    for source, target in ((twice, v_twice), (tail, v_tail)):
        high = target.shape[0]
        small += [(source.at[pl.ds(i * high, high)], target.at[:, pl.ds(i * 128, 128)]) for i in range(2)]
    copies = [
        pltpu.make_async_copy(source, target, local_sem.at[i]) for i, (source, target) in enumerate(small)
    ]
    for copy in copies:
        copy.start()
    barrier = pltpu.get_barrier_semaphore()

    def greet(index):
        pl.semaphore_signal(barrier, inc=1, device_id=device(index), device_id_type=pl.DeviceIdType.MESH)

    for offset in range(1, plane):
        greet(z * plane + peer(offset))
    for distance in range(1, Z):
        greet((z + distance) % Z * plane + p)
    pl.semaphore_wait(barrier, plane - 1 + Z - 1)

    def table_copy(way, distance):
        chunk = z - distance if way == 0 else z + distance
        target = me + plane if way == 0 else me - plane
        return remote(
            table.at[chunk], table.at[chunk], tab_ss.at[way, distance], tab_rs.at[way, distance + 1], target
        )

    def table_wait(way, distance):
        chunk = z - distance if way == 0 else z + distance
        remote(
            table.at[chunk], table.at[chunk], tab_ss.at[way, distance], tab_rs.at[way, distance], me
        ).wait_recv()

    def arrives(way, distance):
        return z >= distance if way == 0 else z <= Z - 1 - distance

    def goes_on(way, distance):
        return ((z >= distance) & (z < Z - 1)) if way == 0 else ((z <= Z - 1 - distance) & (z > 0))

    copies[4].wait()
    copies[5].wait()
    for way in range(2):
        pl.when(goes_on(way, 0))(lambda way=way: table_copy(way, 0).start())
    for i in range(4):
        copies[i].wait()

    found = [
        find_slots(v_rcv_row[...], v_rcv_home[...], rcv_terms),
        find_slots(v_cmp_row[...], v_cmp_home[...], cmp_terms),
    ]
    lane = iota((count, 128), 1)
    req_rows = 2 * Z * plane
    req_iota = iota((req_rows, count), 0)
    wanted = ((req_iota >> 1) & (Z - 1)) * plane + req_iota // (2 * Z)
    slots, slot_rows, owner_rows, rank_hots = [], [], [], []
    request = jnp.zeros((req_rows, 128), F32)
    for kind, (owner, rank, place) in enumerate(found):
        owner_row = as_row(owner)
        slot = owner * pair + (kind * slot_cap + rank)
        rank_hot = lane == rank
        lhs = pick_mask((wanted == owner_row) & ((req_iota & 1) == kind))
        request = request + mm(lhs, jnp.where(rank_hot, place, 0.0).astype(BF))
        slots.append(slot)
        slot_rows.append(as_row(slot))
        owner_rows.append(owner_row)
        rank_hots.append(rank_hot)
    req_send[...] = request.reshape(plane, 2 * Z, 128)
    req_copies = [
        remote(
            req_send.at[peer(offset)], req_recv.at[p], req_ss.at[offset], req_rs.at[p],
            z * plane + peer(offset),
        )
        for offset in range(1, plane)
    ]
    for copy in req_copies:
        copy.start()
    req_recv[pl.ds(p, 1)] = req_send[pl.ds(p, 1)]

    for i in range(6, 16):
        copies[i].wait()

    def spectra(start, stop):
        @pl.loop(start, stop)
        def _(turn):
            here = pl.ds(pl.multiple_of(turn * ROWS, ROWS), ROWS)
            q[here, :], cross[here, :], last[here, :], power[here, :] = spectra_rows(
                v_traces[here, :], v_targets[here, :], v_twice[...], v_even[...], spec_x, spec_t
            )

    turns = count // ROWS
    spectra(0, turns // 4)

    for offset in range(1, plane):
        source = peer(offset)
        remote(
            req_send.at[source], req_recv.at[source], req_ss.at[offset], req_rs.at[source], me
        ).wait_recv()

    cap_bits = slot_cap.bit_length() - 1

    def value_copy(chunk, offset):
        return remote(
            vals.at[chunk, peer(offset)], fetched.at[chunk, p], val_ss.at[chunk, offset],
            val_rs.at[chunk, p], z * plane + peer(offset),
        )

    def serve(chunk):
        request_rows = req_recv[...].reshape(plane * 2 * Z, 128).astype(BF)
        row = iota((width, plane * 2 * Z), 0)
        col = iota((width, plane * 2 * Z), 1)
        kind = (row >> cap_bits) & 1
        expand = pick_mask(col == (row >> (cap_bits + 1)) * (2 * Z) + 2 * chunk + kind)
        wide = mm(expand, request_rows)
        row = iota((width, 128), 0)
        mine = (row & (slot_cap - 1)) == iota((width, 128), 1)
        place = mm(jnp.where(mine, wide, 0.0).astype(BF), jnp.ones((128, 128), BF)).astype(jnp.int32)
        place = place + ((row >> cap_bits) & 1) * rcv_terms
        onehot = jnp.concatenate(
            [pick_mask(iota((width, 128), 1) + base == place) for base in range(0, rows_all, 128)], axis=1
        )
        vals[chunk] = pick_mm(onehot, split2(table[chunk])).reshape(plane, pair, 128)
        for offset in range(1, plane):
            value_copy(chunk, offset).start()
        fetched[chunk, pl.ds(p, 1)] = vals[chunk, pl.ds(p, 1)]
        hot[chunk] = pick_mask(iota((rows_all, width), 0) == as_row(place))

    def take(chunk):
        for offset in range(1, plane):
            source = peer(offset)
            remote(
                vals.at[chunk, source], fetched.at[chunk, source], val_ss.at[chunk, offset],
                val_rs.at[chunk, source], me,
            ).wait_recv()
        mixed[...] += pick_mm(slot_hot[chunk], split2(fetched[chunk].reshape(width, 128)))

    serve(z)
    src_hot = pick_mask(iota((8, count), 0) == v_src_row[...])
    mixed[...] = src_rows(src_hot, v_src_f[...])

    def near(act, distance):
        if distance == 0:
            act(z)
            return
        for way in range(2):
            chunk = z - distance if way == 0 else z + distance
            pl.when(arrives(way, distance))(lambda chunk=chunk: act(chunk))

    marks = [turns // 4, 5 * turns // 8, turns, turns]
    for distance in range(1, Z):
        for way in range(2):
            pl.when(arrives(way, distance))(lambda way=way: table_wait(way, distance))
            if distance < Z - 1:
                pl.when(goes_on(way, distance))(lambda way=way: table_copy(way, distance).start())
        near(serve, distance)
        if distance == 1:
            for chunk in range(Z):
                slot_hot[chunk] = both_hot(slots, chunk * width, width)
        spectra(marks[distance - 1], marks[distance])
        if distance == 2:
            powers = jnp.where(iota((count, 128), 0) < counts[0], power[...], 0.0)
            row = iota((Z * plane * 8, count), 0)
            energy = jnp.zeros((Z * plane * 8, 128), F32)
            for kind in range(2):
                onehot = pick_mask(((row >> 3) == owner_rows[kind]) & ((row & 7) == kind))
                energy = energy + pick_mm(onehot, split2(jnp.where(rank_hots[kind], powers, 0.0)))
            grad_send[:, :, pl.ds(pair, 8), :] = energy.reshape(Z, plane, 8, 128)
            src_energy = pick_mm(src_hot, split2(powers))
            for chunk in range(Z):
                row = iota((width, count), 0) + chunk * width
                slot_hot_t[chunk] = pick_mask((row == slot_rows[0]) | (row == slot_rows[1]))
        near(take, distance - 1)
    near(take, Z - 1)

    grads = gradients(
        mixed[...].astype(BF), q[...], cross[...], last[...], v_twice[...], v_tail[...], v_inverse[...]
    )
    grads = jnp.where(iota((count, 128), 0) < counts[0], grads, 0.0)
    grad_parts = split2(grads)

    order = (3 * (1 - z // 2), (2 + 3 * z) % 5, 1 + z % 2, z)

    def grad_copy(chunk, offset):
        return remote(
            grad_send.at[chunk, peer(offset)], grad_recv.at[chunk, p], grad_ss.at[chunk, offset],
            grad_rs.at[chunk, p], z * plane + peer(offset),
        )

    for chunk in order:
        sent = pick_mm(slot_hot_t[chunk], grad_parts)
        grad_send[chunk, :, pl.ds(0, pair), :] = sent.reshape(plane, pair, 128)
        for offset in range(1, plane):
            grad_copy(chunk, offset).start()
        grad_recv[chunk, pl.ds(p, 1)] = grad_send[chunk, pl.ds(p, 1)]
    src_out[...] = settled_src(v_src_f[...], src_hot, grads, src_energy)

    def part_copy(chunk, way):
        target = me + plane if way == 0 else me - plane
        return remote(
            part.at[chunk], inbox.at[way, chunk], part_ss.at[chunk], part_rs.at[way, chunk], target
        )

    def add_inbox(chunk, way):
        remote(
            part.at[chunk], inbox.at[way, chunk], part_ss.at[chunk], part_rs.at[way, chunk], me
        ).wait_recv()
        part[chunk] = part[chunk] + inbox[way, chunk]

    for step, chunk in enumerate(order):
        for offset in range(1, plane):
            source = peer(offset)
            remote(
                grad_send.at[chunk, source], grad_recv.at[chunk, source], grad_ss.at[chunk, offset],
                grad_rs.at[chunk, source], me,
            ).wait_recv()
        onehot = hot[chunk]
        got = split2(grad_recv[chunk, :, pl.ds(0, pair), :].reshape(width, 128))
        part[chunk, pl.ds(0, rows_all)] = pick_mm(onehot, got)
        energy = grad_recv[chunk, :, pl.ds(pair, 8), :].reshape(plane * 8, 128)
        row, col = iota((plane * 8, width), 0), iota((plane * 8, width), 1)
        spread = pick_mask(
            ((row >> 3) == (col >> (cap_bits + 1))) & ((row & 7) == ((col >> cap_bits) & 1))
        )
        wide = mm_t(split2(energy), spread)
        mine = (iota((256, width), 1) & (slot_cap - 1)) == (iota((256, width), 0) & 127)
        energy = jnp.sum(jnp.where(mine, wide, 0.0), axis=0, keepdims=True)
        high = energy.astype(BF).astype(F32)
        energy = jnp.where(iota((8, width), 0) < 4, high, energy - high).astype(BF)
        energy = lax.dot_general(energy, onehot, (((1,), (1,)), ((), ())), preferred_element_type=F32)
        energy = energy[0:1] + energy[4:5]
        lines8 = iota((8, 128), 0)
        packed = jnp.zeros((8, 128), F32)
        for i in range(rows_all // 128):
            packed = packed + jnp.where(lines8 == i, energy[:, i * 128 : (i + 1) * 128], 0.0)
        part[chunk, pl.ds(rows_all, 8)] = packed
        pl.when((chunk >= z) & (z > 0))(lambda chunk=chunk: add_inbox(chunk, 0))
        pl.when((chunk <= z) & (z < Z - 1))(lambda chunk=chunk: add_inbox(chunk, 1))
        if step < Z - 1:
            pl.when(chunk > z)(lambda chunk=chunk: part_copy(chunk, 0).start())
            pl.when(chunk < z)(lambda chunk=chunk: part_copy(chunk, 1).start())

    packed = part[z, pl.ds(rows_all, 8)]
    for i in range(rows_all // 128):
        energy = jnp.transpose(jnp.broadcast_to(packed[i : i + 1, :], (128, 128)))
        here = pl.ds(i * 128, 128)
        updated = table[z, here] - STEP * part[z, here] / jnp.maximum(energy, 1.0)
        if i * 128 < rcv_terms:
            rcv_out[here, :] = updated
        else:
            cmp_out[pl.ds(i * 128 - rcv_terms, 128), :] = updated

    for copy in req_copies:
        copy.wait_send()
    for distance in range(Z - 1):
        for way in range(2):
            pl.when(goes_on(way, distance))(lambda way=way: table_copy(way, distance).wait_send())
    for chunk in range(Z):
        for offset in range(1, plane):
            value_copy(chunk, offset).wait_send()
            grad_copy(chunk, offset).wait_send()
        pl.when(z != chunk)(lambda chunk=chunk: part_copy(chunk, 0).wait_send())


def body(
    traces, targets, src_local, rcv_term, cmp_term, rcv_home, cmp_home, counts,
    src_filters, rcv_filters, cmp_filters,
):
    trace_rows, samples = traces.shape
    taps = src_filters.shape[1]
    device_count = lax.axis_size(AXES)
    lines = lax.axis_size("line")
    slot_cap = max(2, 2 * trace_rows // device_count)
    plane = device_count // Z
    pair = 2 * slot_cap
    blocks = samples // taps
    terms = (rcv_filters.shape[0], cmp_filters.shape[0])
    rows_all = sum(terms)
    tables = tuple(jnp.asarray(table) for table in spectral_tables(taps))
    shape = jax.ShapeDtypeStruct
    vmem, sem = pltpu.VMEM, pltpu.SemaphoreType.DMA
    operands = (
        traces, targets, src_local.reshape(1, -1), rcv_term.reshape(1, -1), cmp_term.reshape(1, -1),
        rcv_home.reshape(-1, 128), cmp_home.reshape(-1, 128),
        src_filters, rcv_filters, cmp_filters, *tables,
    )
    held = [vmem(x.shape, x.dtype) for x in operands[:8]]
    held += [vmem((x.shape[0] * 128 // w, w), x.dtype) for x, w in zip(tables, (256, 128, 256, 128))]
    return pl.pallas_call(
        functools.partial(fused_kernel, (lines, plane, slot_cap, terms)),
        out_shape=tuple(shape(x.shape, F32) for x in (src_filters, rcv_filters, cmp_filters)),
        in_specs=[pl.BlockSpec(memory_space=pltpu.SMEM)]
        + [pl.BlockSpec(memory_space=pltpu.HBM)] * len(operands),
        out_specs=(pl.BlockSpec(memory_space=pltpu.VMEM),) * 3,
        scratch_shapes=held
        + [
            vmem((Z, rows_all, 128), F32),
            vmem((plane, 2 * Z, 128), F32),
            vmem((plane, 2 * Z, 128), F32),
            vmem((Z, plane, pair, 128), F32),
            vmem((Z, plane, pair, 128), F32),
            vmem((Z, rows_all, plane * pair), BF),
            vmem((Z, plane, pair + 8, 128), F32),
            vmem((Z, plane, pair + 8, 128), F32),
            vmem((Z, rows_all + 8, 128), F32),
            vmem((2, Z, rows_all + 8, 128), F32),
            vmem((trace_rows, taps), F32),
            vmem((Z, trace_rows, plane * pair), BF),
            vmem((Z, plane * pair, trace_rows), BF),
            vmem((trace_rows, taps), F32),
            vmem((trace_rows, 2 * taps), F32),
            vmem((trace_rows, 2 * taps), F32),
            vmem((trace_rows, 128), F32),
            vmem((ROWS * blocks, 2 * taps), F32),
            vmem((ROWS * blocks, 2 * taps), F32),
            sem((16,)),
            sem((plane,)), sem((plane,)),
            sem((2, Z)), sem((2, Z + 1)),
            sem((Z, plane)), sem((Z, plane)),
            sem((Z, plane)), sem((Z, plane)),
            sem((Z,)), sem((2, Z)),
        ],
        compiler_params=pltpu.CompilerParams(
            vmem_limit_bytes=VMEM_LIMIT, collective_id=0, has_side_effects=True
        ),
        cost_estimate=pl.CostEstimate(
            flops=16 * trace_rows * samples * taps, bytes_accessed=6 * 2**20, transcendentals=0
        ),
    )(counts, *operands)


def solution(mesh):
    rows, flat = P(AXES, None), P(AXES)
    return jax.shard_map(
        body,
        mesh=mesh,
        in_specs=(rows, rows, flat, flat, flat, P(), P(), flat, rows, rows, rows),
        out_specs=(rows, rows, rows),
        check_vma=False,
    )
```

```python
import functools

import jax
import jax.numpy as jnp
import numpy as np
from jax import lax
from jax.experimental import pallas as pl
from jax.experimental.pallas import tpu as pltpu
from jax.sharding import PartitionSpec as P

STEP = 0.5
BF = jnp.bfloat16
F32 = jnp.float32
AXES = ("shot", "line")
ROWS = 64
Z = 4
VMEM_LIMIT = 60 * 1024 * 1024


def halves(matrix):
    high = matrix.astype(jnp.bfloat16)
    low = (matrix - high.astype(np.float64)).astype(jnp.bfloat16)
    return high, low


def spectral_tables(taps):
    span = 2 * taps
    theta = 2 * np.pi * (np.arange(taps) + 0.5) / span
    angle = np.arange(span)[:, None] * theta[None, :]
    forward = np.concatenate([np.cos(angle), -np.sin(angle)], axis=1)
    inverse = forward.T / taps
    even = 2 * np.cos(angle[:taps])
    even[0] = 1.0
    fwd_high, fwd_low = halves(forward[:taps])
    twice = np.concatenate([fwd_high, fwd_low], axis=0)

    def triple(matrix):
        high, low = halves(matrix)
        return np.concatenate([high, high, low], axis=0)

    def tall(matrix):
        return np.concatenate([matrix[:, :128], matrix[:, 128:]], axis=0)

    return (
        tall(twice),
        triple(inverse[:, :taps] @ even),
        tall(triple(inverse[:, taps:] @ forward[taps:])),
        triple(inverse[:, :taps]),
    )


def mm(left, right):
    return jnp.dot(left, right, preferred_element_type=F32)


def mm_t(left, right):
    return lax.dot_general(left, right, (((0,), (0,)), ((), ())), preferred_element_type=F32)


def split2(value):
    high = value.astype(BF)
    return jnp.concatenate([high, (value - high.astype(F32)).astype(BF)], axis=1)


def folded(wide):
    half = wide.shape[1] // 2
    return wide[:, :half] + wide[:, half:]


def pick_mm(onehot, parts):
    return folded(mm(onehot, parts))


def fine_mm(value, table):
    high = value.astype(BF)
    low = (value - high.astype(F32)).astype(BF)
    return mm(jnp.concatenate([high, low, high], axis=1), table)


def iota(shape, dim):
    return lax.broadcasted_iota(jnp.int32, shape, dim)


def pick_mask(condition):
    return jnp.where(condition, 1.0, 0.0).astype(BF)


def row_to_lanes(row):
    return jnp.transpose(jnp.broadcast_to(row, (128, row.shape[1])))


def find_slots(term_row, home, terms_dev):
    count = term_row.shape[1]
    shift = terms_dev.bit_length() - 1
    lane = iota((count, 128), 1)
    term = row_to_lanes(term_row)
    chunks = home.shape[0]
    high_term, low_term = term >> 7, term & 127
    if chunks <= 128:
        onehot = pick_mask(lane[:, :chunks] == high_term[:, :chunks])
    else:
        onehot = jnp.concatenate(
            [pick_mask(lane + base == high_term) for base in range(0, chunks, 128)], axis=1
        )
    ones = jnp.ones((128, 128), BF)
    here = lane == low_term
    high = mm(onehot, (home >> 7).astype(F32).astype(BF))
    low = mm(onehot, (home & 127).astype(F32).astype(BF))
    high = mm(jnp.where(here, high, 0.0).astype(BF), ones)
    low = mm(jnp.where(here, low, 0.0).astype(BF), ones)
    row = high.astype(jnp.int32) * 128 + low.astype(jnp.int32)
    owner = row >> shift
    place = (row & (terms_dev - 1)).astype(F32)
    earlier = pick_mask(iota((count, count), 1) < iota((count, count), 0))
    before = mm(earlier, pick_mask(lane == owner))
    rank = mm(jnp.where(lane == owner, before, 0.0).astype(BF), ones).astype(jnp.int32)
    return owner, rank, place


def as_row(lanes):
    return jnp.transpose(lanes)[0:1, :]


def both_hot(slots, base, width):
    lane = iota(slots[0].shape, 1)
    parts = []
    for start in range(0, width, 128):
        here = lane + (base + start)
        parts.append(pick_mask((here == slots[0]) | (here == slots[1])))
    return jnp.concatenate(parts, axis=1)


def spectra_rows(trace_rows, target_rows, twice, even, spec_x, spec_t):
    taps = twice.shape[0] // 2
    rows, samples = trace_rows.shape
    blocks = samples // taps

    def stacked(value):
        tall = jnp.concatenate([value[:, b * taps : (b + 1) * taps] for b in range(blocks)], axis=0)
        return jnp.concatenate([tall, tall], axis=1)

    spec_x[...] = mm(stacked(trace_rows), twice)
    spec_t[...] = mm(stacked(target_rows), twice)
    sign = 1.0 - 2.0 * (iota((16, taps), 1) & 1).astype(F32)
    out = []
    for start in range(0, rows, 16):
        c0r = c0i = c1r = c1i = p0 = p1r = p1i = jnp.zeros((16, taps), F32)
        xr0 = xi0 = None
        for b in range(blocks):
            here = pl.ds(b * rows + start, 16)
            xr, xi = spec_x[here, :taps], spec_x[here, taps:]
            tr, ti = spec_t[here, :taps], spec_t[here, taps:]
            c0r += xr * tr + xi * ti
            c0i += xr * ti - xi * tr
            p0 += xr * xr + xi * xi
            if b:
                c1r += xr0 * tr + xi0 * ti
                c1i += xr0 * ti - xi0 * tr
                p1r += xr0 * xr + xi0 * xi
                p1i += xr0 * xi - xi0 * xr
            xr0, xi0 = xr, xi
        power = jnp.sum(p0, axis=1, keepdims=True) * (1.0 / taps)
        out.append(
            (
                jnp.concatenate([p0 + sign * p1i, -sign * p1r], axis=1),
                jnp.concatenate([c0r + sign * c1i, c0i - sign * c1r], axis=1),
                jnp.concatenate([xr0, xi0], axis=1),
                jnp.broadcast_to(power, (16, 128)),
            )
        )
    auto, cross, last, power = (jnp.concatenate(parts, axis=0) for parts in zip(*out))
    return fine_mm(auto, even), cross, last, power


def gradients(mixed, q, cross, last, twice, tail, inverse):
    taps = q.shape[1]
    fs = mm(jnp.concatenate([mixed, mixed], axis=1), twice)
    fr, fi = fs[:, :taps], fs[:, taps:]
    xr, xi = last[:, :taps], last[:, taps:]
    over = fine_mm(jnp.concatenate([xr * fr - xi * fi, xr * fi + xi * fr], axis=1), tail)
    yr, yi = over[:, :taps], over[:, taps:]
    gr = q * fr - cross[:, :taps] - (xr * yr + xi * yi)
    gi = q * fi - cross[:, taps:] - (xr * yi - xi * yr)
    return fine_mm(jnp.concatenate([gr, gi], axis=1), inverse)


def settled_src(filters, here, grads, energy):
    missing = jnp.zeros((8 - filters.shape[0], filters.shape[1]), F32)
    sums = pick_mm(here, split2(grads))
    return jnp.concatenate([filters, missing], axis=0) - STEP * sums / jnp.maximum(energy, 1.0)


def src_rows(here, src_filters):
    missing = jnp.zeros((8 - src_filters.shape[0], src_filters.shape[1]), F32)
    return folded(mm_t(here, split2(jnp.concatenate([src_filters, missing], axis=0))))


def fused_kernel(
    sizes, counts, traces, targets, src_row, rcv_row, cmp_row, rcv_home, cmp_home,
    src_f, rcv_f, cmp_f, twice, even, tail, inverse,
    out,
    v_traces, v_targets, v_src_row, v_rcv_row, v_cmp_row, v_rcv_home, v_cmp_home,
    v_src_f, v_twice, v_even, v_tail, v_inverse,
    table, req_send, req_recv, vals, fetched, hot, grad_send, grad_recv, part, inbox,
    mixed, slot_hot, slot_hot_t, q, cross, last, power, spec_x, spec_t,
    local_sem, req_ss, req_rs, tab_ss, tab_rs, val_ss, val_rs, grad_ss, grad_rs, part_ss, part_rs,
):
    lines, plane, slot_cap, terms = sizes
    rcv_terms, cmp_terms = terms
    rows_all = rcv_terms + cmp_terms
    pair = 2 * slot_cap
    width = plane * pair
    count = v_traces.shape[0]
    me = lax.axis_index("shot") * lines + lax.axis_index("line")
    z, p = me // plane, me % plane

    def device(index):
        return (index // lines, index % lines)

    def peer(offset):
        return (p + offset) % plane

    def remote(source, target, send, recv, index):
        return pltpu.make_async_remote_copy(
            src_ref=source, dst_ref=target, send_sem=send, recv_sem=recv,
            device_id=device(index), device_id_type=pl.DeviceIdType.MESH,
        )

    barrier = pltpu.get_barrier_semaphore()

    def greet(index):
        pl.semaphore_signal(barrier, inc=1, device_id=device(index), device_id_type=pl.DeviceIdType.MESH)

    for distance in range(1, Z):
        greet((z + distance) % Z * plane + p)
    for offset in range(1, plane):
        greet(z * plane + peer(offset))

    small = [
        (rcv_row, v_rcv_row), (cmp_row, v_cmp_row), (rcv_home, v_rcv_home), (cmp_home, v_cmp_home),
        (rcv_f, table.at[z, pl.ds(0, rcv_terms)]), (cmp_f, table.at[z, pl.ds(rcv_terms, cmp_terms)]),
        (src_row, v_src_row), (src_f, v_src_f), (even, v_even), (inverse, v_inverse),
        (traces, v_traces), (targets, v_targets),
    ]
    for source, target in ((twice, v_twice), (tail, v_tail)):
        high = target.shape[0]
        small += [(source.at[pl.ds(i * high, high)], target.at[:, pl.ds(i * 128, 128)]) for i in range(2)]
    copies = [
        pltpu.make_async_copy(source, target, local_sem.at[i]) for i, (source, target) in enumerate(small)
    ]
    for copy in copies:
        copy.start()
    pl.semaphore_wait(barrier, plane - 1 + Z - 1)

    half = rows_all // 2

    def table_copy(way, distance, piece):
        chunk = z - distance if way == 0 else z + distance
        target = me + plane if way == 0 else me - plane
        rows = table.at[chunk, pl.ds(piece * half, half)]
        return remote(
            rows, rows, tab_ss.at[way, distance, piece], tab_rs.at[way, distance + 1, piece], target
        )

    def table_wait(way, distance, piece):
        chunk = z - distance if way == 0 else z + distance
        rows = table.at[chunk, pl.ds(piece * half, half)]
        remote(
            rows, rows, tab_ss.at[way, distance, piece], tab_rs.at[way, distance, piece], me
        ).wait_recv()

    def arrives(way, distance):
        return z >= distance if way == 0 else z <= Z - 1 - distance

    def goes_on(way, distance):
        return ((z >= distance) & (z < Z - 1)) if way == 0 else ((z <= Z - 1 - distance) & (z > 0))

    copies[4].wait()
    copies[5].wait()
    for piece in range(2):
        for way in range(2):
            pl.when(goes_on(way, 0))(lambda way=way, piece=piece: table_copy(way, 0, piece).start())
    for i in range(4):
        copies[i].wait()

    found = [
        find_slots(v_rcv_row[...], v_rcv_home[...], rcv_terms),
        find_slots(v_cmp_row[...], v_cmp_home[...], cmp_terms),
    ]
    lane = iota((count, 128), 1)
    req_rows = 2 * Z * plane
    req_iota = iota((req_rows, count), 0)
    wanted = ((req_iota >> 1) & (Z - 1)) * plane + req_iota // (2 * Z)
    slots, slot_rows, owner_rows, rank_hots = [], [], [], []
    request = jnp.zeros((req_rows, 128), F32)
    for kind, (owner, rank, place) in enumerate(found):
        owner_row = as_row(owner)
        slot = owner * pair + (kind * slot_cap + rank)
        rank_hot = lane == rank
        lhs = pick_mask((wanted == owner_row) & ((req_iota & 1) == kind))
        request = request + mm(lhs, jnp.where(rank_hot, place, 0.0).astype(BF))
        slots.append(slot)
        slot_rows.append(as_row(slot))
        owner_rows.append(owner_row)
        rank_hots.append(rank_hot)
    req_send[...] = request.reshape(plane, 2 * Z, 128)
    req_copies = [
        remote(
            req_send.at[peer(offset)], req_recv.at[p], req_ss.at[offset], req_rs.at[p],
            z * plane + peer(offset),
        )
        for offset in range(1, plane)
    ]
    for copy in req_copies:
        copy.start()
    req_recv[pl.ds(p, 1)] = req_send[pl.ds(p, 1)]

    for i in range(6, 16):
        copies[i].wait()

    def spectra(start, stop):
        @pl.loop(start, stop)
        def _(turn):
            here = pl.ds(pl.multiple_of(turn * ROWS, ROWS), ROWS)
            q[here, :], cross[here, :], last[here, :], power[here, :] = spectra_rows(
                v_traces[here, :], v_targets[here, :], v_twice[...], v_even[...], spec_x, spec_t
            )

    turns = count // ROWS
    spectra(0, turns // 4)

    for offset in range(1, plane):
        source = peer(offset)
        remote(
            req_send.at[source], req_recv.at[source], req_ss.at[offset], req_rs.at[source], me
        ).wait_recv()

    cap_bits = slot_cap.bit_length() - 1

    def value_copy(chunk, offset):
        return remote(
            vals.at[chunk, peer(offset)], fetched.at[chunk, p], val_ss.at[chunk, offset],
            val_rs.at[chunk, p], z * plane + peer(offset),
        )

    def serve(chunk):
        request_rows = req_recv[...].reshape(plane * 2 * Z, 128).astype(BF)
        row = iota((width, plane * 2 * Z), 0)
        col = iota((width, plane * 2 * Z), 1)
        kind = (row >> cap_bits) & 1
        expand = pick_mask(col == (row >> (cap_bits + 1)) * (2 * Z) + 2 * chunk + kind)
        wide = mm(expand, request_rows)
        row = iota((width, 128), 0)
        mine = (row & (slot_cap - 1)) == iota((width, 128), 1)
        place = mm(jnp.where(mine, wide, 0.0).astype(BF), jnp.ones((128, 128), BF)).astype(jnp.int32)
        place = place + ((row >> cap_bits) & 1) * rcv_terms
        onehot = jnp.concatenate(
            [pick_mask(iota((width, 128), 1) + base == place) for base in range(0, rows_all, 128)], axis=1
        )
        vals[chunk] = pick_mm(onehot, split2(table[chunk])).reshape(plane, pair, 128)
        for offset in range(1, plane):
            value_copy(chunk, offset).start()
        fetched[chunk, pl.ds(p, 1)] = vals[chunk, pl.ds(p, 1)]
        hot[chunk] = pick_mask(iota((rows_all, width), 0) == as_row(place))

    def take(chunk):
        for offset in range(1, plane):
            source = peer(offset)
            remote(
                vals.at[chunk, source], fetched.at[chunk, source], val_ss.at[chunk, offset],
                val_rs.at[chunk, source], me,
            ).wait_recv()
        mixed[...] += pick_mm(slot_hot[chunk], split2(fetched[chunk].reshape(width, 128)))

    serve(z)
    src_hot = pick_mask(iota((8, count), 0) == v_src_row[...])
    mixed[...] = src_rows(src_hot, v_src_f[...])

    def near(act, distance):
        if distance == 0:
            act(z)
            return
        for way in range(2):
            chunk = z - distance if way == 0 else z + distance
            pl.when(arrives(way, distance))(lambda chunk=chunk: act(chunk))

    marks = [turns // 4, 5 * turns // 8, turns, turns]
    for distance in range(1, Z):
        for piece in range(2):
            for way in range(2):
                pl.when(arrives(way, distance))(lambda way=way, piece=piece: table_wait(way, distance, piece))
                if distance < Z - 1:
                    pl.when(goes_on(way, distance))(
                        lambda way=way, piece=piece: table_copy(way, distance, piece).start()
                    )
        near(serve, distance)
        if distance == 1:
            for chunk in range(Z):
                slot_hot[chunk] = both_hot(slots, chunk * width, width)
        spectra(marks[distance - 1], marks[distance])
        if distance == 2:
            powers = jnp.where(iota((count, 128), 0) < counts[0], power[...], 0.0)
            row = iota((Z * plane * 8, count), 0)
            energy = jnp.zeros((Z * plane * 8, 128), F32)
            for kind in range(2):
                onehot = pick_mask(((row >> 3) == owner_rows[kind]) & ((row & 7) == kind))
                energy = energy + pick_mm(onehot, split2(jnp.where(rank_hots[kind], powers, 0.0)))
            grad_send[:, :, pl.ds(pair, 8), :] = energy.reshape(Z, plane, 8, 128)
            src_energy = pick_mm(src_hot, split2(powers))
            for chunk in range(Z):
                row = iota((width, count), 0) + chunk * width
                slot_hot_t[chunk] = pick_mask((row == slot_rows[0]) | (row == slot_rows[1]))
        near(take, distance - 1)
    near(take, Z - 1)

    grads = gradients(
        mixed[...].astype(BF), q[...], cross[...], last[...], v_twice[...], v_tail[...], v_inverse[...]
    )
    grads = jnp.where(iota((count, 128), 0) < counts[0], grads, 0.0)
    grad_parts = split2(grads)

    order = (3 * (1 - z // 2), (2 + 3 * z) % 5, 1 + z % 2, z)

    def grad_copy(chunk, offset):
        return remote(
            grad_send.at[chunk, peer(offset)], grad_recv.at[chunk, p], grad_ss.at[chunk, offset],
            grad_rs.at[chunk, p], z * plane + peer(offset),
        )

    for chunk in order:
        sent = pick_mm(slot_hot_t[chunk], grad_parts)
        grad_send[chunk, :, pl.ds(0, pair), :] = sent.reshape(plane, pair, 128)
        for offset in range(1, plane):
            grad_copy(chunk, offset).start()
        grad_recv[chunk, pl.ds(p, 1)] = grad_send[chunk, pl.ds(p, 1)]
    out[pl.ds(rows_all, 8)] = settled_src(v_src_f[...], src_hot, grads, src_energy)

    cut = rows_all // 16 * 8
    spans = (pl.ds(0, cut), pl.ds(cut, rows_all + 8 - cut))

    def part_copy(chunk, way, piece):
        target = me + plane if way == 0 else me - plane
        rows = spans[piece]
        return remote(
            part.at[chunk, rows], inbox.at[way, chunk, rows], part_ss.at[chunk, piece],
            part_rs.at[way, chunk, piece], target,
        )

    def add_inbox(chunk, way, piece):
        rows = spans[piece]
        remote(
            part.at[chunk, rows], inbox.at[way, chunk, rows], part_ss.at[chunk, piece],
            part_rs.at[way, chunk, piece], me,
        ).wait_recv()
        part[chunk, rows] = part[chunk, rows] + inbox[way, chunk, rows]

    for step, chunk in enumerate(order):
        for offset in range(1, plane):
            source = peer(offset)
            remote(
                grad_send.at[chunk, source], grad_recv.at[chunk, source], grad_ss.at[chunk, offset],
                grad_rs.at[chunk, source], me,
            ).wait_recv()
        onehot = hot[chunk]
        got = split2(grad_recv[chunk, :, pl.ds(0, pair), :].reshape(width, 128))
        part[chunk, pl.ds(0, rows_all)] = pick_mm(onehot, got)
        energy = grad_recv[chunk, :, pl.ds(pair, 8), :].reshape(plane * 8, 128)
        row, col = iota((plane * 8, width), 0), iota((plane * 8, width), 1)
        spread = pick_mask(
            ((row >> 3) == (col >> (cap_bits + 1))) & ((row & 7) == ((col >> cap_bits) & 1))
        )
        wide = mm_t(split2(energy), spread)
        mine = (iota((256, width), 1) & (slot_cap - 1)) == (iota((256, width), 0) & 127)
        energy = jnp.sum(jnp.where(mine, wide, 0.0), axis=0, keepdims=True)
        high = energy.astype(BF).astype(F32)
        energy = jnp.where(iota((8, width), 0) < 4, high, energy - high).astype(BF)
        energy = lax.dot_general(energy, onehot, (((1,), (1,)), ((), ())), preferred_element_type=F32)
        energy = energy[0:1] + energy[4:5]
        lines8 = iota((8, 128), 0)
        packed = jnp.zeros((8, 128), F32)
        for i in range(rows_all // 128):
            packed = packed + jnp.where(lines8 == i, energy[:, i * 128 : (i + 1) * 128], 0.0)
        part[chunk, pl.ds(rows_all, 8)] = packed
        for piece in range(2):
            def pass_on(way, chunk=chunk, piece=piece):
                pl.when(z > 0 if way == 0 else z < Z - 1)(lambda: add_inbox(chunk, way, piece))
                if step < Z - 1:
                    part_copy(chunk, way, piece).start()

            pl.when(chunk >= z)(lambda: pass_on(0))
            pl.when(chunk <= z)(lambda: pass_on(1))

    packed = part[z, pl.ds(rows_all, 8)]
    for i in range(rows_all // 128):
        energy = jnp.transpose(jnp.broadcast_to(packed[i : i + 1, :], (128, 128)))
        here = pl.ds(i * 128, 128)
        updated = table[z, here] - STEP * part[z, here] / jnp.maximum(energy, 1.0)
        out[here, :] = updated

    for copy in req_copies:
        copy.wait_send()
    for distance in range(Z - 1):
        for way in range(2):
            for piece in range(2):
                pl.when(goes_on(way, distance))(
                    lambda way=way, piece=piece: table_copy(way, distance, piece).wait_send()
                )
    for chunk in range(Z):
        for offset in range(1, plane):
            value_copy(chunk, offset).wait_send()
            grad_copy(chunk, offset).wait_send()
        for piece in range(2):
            pl.when(z != chunk)(lambda chunk=chunk, piece=piece: part_copy(chunk, 0, piece).wait_send())


def deliver_kernel(updated, src_out, rcv_out, cmp_out, sems):
    rcv_terms, cmp_terms = rcv_out.shape[0], cmp_out.shape[0]
    spans = (
        (rcv_terms + cmp_terms, src_out.shape[0], src_out),
        (0, rcv_terms, rcv_out),
        (rcv_terms, cmp_terms, cmp_out),
    )
    copies = [
        pltpu.make_async_copy(updated.at[pl.ds(start, size)], target, sems.at[i])
        for i, (start, size, target) in enumerate(spans)
    ]
    for copy in copies:
        copy.start()
    for copy in copies:
        copy.wait()


def body(
    traces, targets, src_local, rcv_term, cmp_term, rcv_home, cmp_home, counts,
    src_filters, rcv_filters, cmp_filters,
):
    trace_rows, samples = traces.shape
    taps = src_filters.shape[1]
    device_count = lax.axis_size(AXES)
    lines = lax.axis_size("line")
    slot_cap = max(2, 2 * trace_rows // device_count)
    plane = device_count // Z
    pair = 2 * slot_cap
    blocks = samples // taps
    terms = (rcv_filters.shape[0], cmp_filters.shape[0])
    rows_all = sum(terms)
    tables = tuple(jnp.asarray(table) for table in spectral_tables(taps))
    shape = jax.ShapeDtypeStruct
    vmem, sem = pltpu.VMEM, pltpu.SemaphoreType.DMA
    operands = (
        traces, targets, src_local.reshape(1, -1), rcv_term.reshape(1, -1), cmp_term.reshape(1, -1),
        rcv_home.reshape(-1, 128), cmp_home.reshape(-1, 128),
        src_filters, rcv_filters, cmp_filters, *tables,
    )
    held = [vmem(x.shape, x.dtype) for x in operands[:8]]
    held += [vmem((x.shape[0] * 128 // w, w), x.dtype) for x, w in zip(tables, (256, 128, 256, 128))]
    updated = pl.pallas_call(
        functools.partial(fused_kernel, (lines, plane, slot_cap, terms)),
        out_shape=shape((rows_all + 8, taps), F32),
        in_specs=[pl.BlockSpec(memory_space=pltpu.SMEM)]
        + [pl.BlockSpec(memory_space=pltpu.HBM)] * len(operands),
        out_specs=pl.BlockSpec(memory_space=pltpu.VMEM),
        scratch_shapes=held
        + [
            vmem((Z, rows_all, 128), F32),
            vmem((plane, 2 * Z, 128), F32),
            vmem((plane, 2 * Z, 128), F32),
            vmem((Z, plane, pair, 128), F32),
            vmem((Z, plane, pair, 128), F32),
            vmem((Z, rows_all, plane * pair), BF),
            vmem((Z, plane, pair + 8, 128), F32),
            vmem((Z, plane, pair + 8, 128), F32),
            vmem((Z, rows_all + 8, 128), F32),
            vmem((2, Z, rows_all + 8, 128), F32),
            vmem((trace_rows, taps), F32),
            vmem((Z, trace_rows, plane * pair), BF),
            vmem((Z, plane * pair, trace_rows), BF),
            vmem((trace_rows, taps), F32),
            vmem((trace_rows, 2 * taps), F32),
            vmem((trace_rows, 2 * taps), F32),
            vmem((trace_rows, 128), F32),
            vmem((ROWS * blocks, 2 * taps), F32),
            vmem((ROWS * blocks, 2 * taps), F32),
            sem((16,)),
            sem((plane,)), sem((plane,)),
            sem((2, Z, 2)), sem((2, Z + 1, 2)),
            sem((Z, plane)), sem((Z, plane)),
            sem((Z, plane)), sem((Z, plane)),
            sem((Z, 2)), sem((2, Z, 2)),
        ],
        compiler_params=pltpu.CompilerParams(
            vmem_limit_bytes=VMEM_LIMIT, collective_id=0, has_side_effects=True
        ),
        cost_estimate=pl.CostEstimate(
            flops=16 * trace_rows * samples * taps, bytes_accessed=6 * 2**20, transcendentals=0
        ),
    )(counts, *operands)
    anywhere = pl.BlockSpec(memory_space=pl.ANY)
    return pl.pallas_call(
        deliver_kernel,
        out_shape=tuple(shape(x.shape, F32) for x in (src_filters, rcv_filters, cmp_filters)),
        in_specs=[anywhere],
        out_specs=(anywhere,) * 3,
        scratch_shapes=[sem((3,))],
        compiler_params=pltpu.CompilerParams(vmem_limit_bytes=VMEM_LIMIT),
    )(updated)


def solution(mesh):
    rows, flat = P(AXES, None), P(AXES)
    return jax.shard_map(
        body,
        mesh=mesh,
        in_specs=(rows, rows, flat, flat, flat, P(), P(), flat, rows, rows, rows),
        out_specs=(rows, rows, rows),
        check_vma=False,
    )
```

```python
import functools

import jax
import jax.numpy as jnp
import numpy as np
from jax import lax
from jax.experimental import pallas as pl
from jax.experimental.pallas import tpu as pltpu
from jax.sharding import PartitionSpec as P

STEP = 0.5
BF = jnp.bfloat16
F32 = jnp.float32
AXES = ("shot", "line")
ROWS = 64
PIECES = 3
Z = 4
VMEM_LIMIT = 60 * 1024 * 1024


def halves(matrix):
    high = matrix.astype(jnp.bfloat16)
    low = (matrix - high.astype(np.float64)).astype(jnp.bfloat16)
    return high, low


def spectral_tables(taps):
    span = 2 * taps
    theta = 2 * np.pi * (np.arange(taps) + 0.5) / span
    angle = np.arange(span)[:, None] * theta[None, :]
    forward = np.concatenate([np.cos(angle), -np.sin(angle)], axis=1)
    inverse = forward.T / taps
    even = 2 * np.cos(angle[:taps])
    even[0] = 1.0
    fwd_high, fwd_low = halves(forward[:taps])
    twice = np.concatenate([fwd_high, fwd_low], axis=0)

    def triple(matrix):
        high, low = halves(matrix)
        return np.concatenate([high, high, low], axis=0)

    def tall(matrix):
        return np.concatenate([matrix[:, :128], matrix[:, 128:]], axis=0)

    return (
        tall(twice),
        triple(inverse[:, :taps] @ even),
        tall(triple(inverse[:, taps:] @ forward[taps:])),
        triple(inverse[:, :taps]),
    )


def mm(left, right):
    return jnp.dot(left, right, preferred_element_type=F32)


def mm_t(left, right):
    return lax.dot_general(left, right, (((0,), (0,)), ((), ())), preferred_element_type=F32)


def split2(value):
    high = value.astype(BF)
    return jnp.concatenate([high, (value - high.astype(F32)).astype(BF)], axis=1)


def folded(wide):
    half = wide.shape[1] // 2
    return wide[:, :half] + wide[:, half:]


def pick_mm(onehot, parts):
    return folded(mm(onehot, parts))


def fine_mm(value, table):
    high = value.astype(BF)
    low = (value - high.astype(F32)).astype(BF)
    return mm(jnp.concatenate([high, low, high], axis=1), table)


def iota(shape, dim):
    return lax.broadcasted_iota(jnp.int32, shape, dim)


def pick_mask(condition):
    return jnp.where(condition, 1.0, 0.0).astype(BF)


def row_to_lanes(row):
    return jnp.transpose(jnp.broadcast_to(row, (128, row.shape[1])))


def find_slots(term_row, home, terms_dev):
    count = term_row.shape[1]
    shift = terms_dev.bit_length() - 1
    lane = iota((count, 128), 1)
    term = row_to_lanes(term_row)
    chunks = home.shape[0]
    high_term, low_term = term >> 7, term & 127
    if chunks <= 128:
        onehot = pick_mask(lane[:, :chunks] == high_term[:, :chunks])
    else:
        onehot = jnp.concatenate(
            [pick_mask(lane + base == high_term) for base in range(0, chunks, 128)], axis=1
        )
    ones = jnp.ones((128, 128), BF)
    here = lane == low_term
    high = mm(onehot, (home >> 7).astype(F32).astype(BF))
    low = mm(onehot, (home & 127).astype(F32).astype(BF))
    high = mm(jnp.where(here, high, 0.0).astype(BF), ones)
    low = mm(jnp.where(here, low, 0.0).astype(BF), ones)
    row = high.astype(jnp.int32) * 128 + low.astype(jnp.int32)
    owner = row >> shift
    place = (row & (terms_dev - 1)).astype(F32)
    earlier = pick_mask(iota((count, count), 1) < iota((count, count), 0))
    before = mm(earlier, pick_mask(lane == owner))
    rank = mm(jnp.where(lane == owner, before, 0.0).astype(BF), ones).astype(jnp.int32)
    return owner, rank, place


def as_row(lanes):
    return jnp.transpose(lanes)[0:1, :]


def both_hot(slots, base, width):
    lane = iota(slots[0].shape, 1)
    parts = []
    for start in range(0, width, 128):
        here = lane + (base + start)
        parts.append(pick_mask((here == slots[0]) | (here == slots[1])))
    return jnp.concatenate(parts, axis=1)


def spectra_rows(trace_rows, target_rows, twice, even, spec_x, spec_t):
    taps = twice.shape[0] // 2
    rows, samples = trace_rows.shape
    blocks = samples // taps

    def stacked(value):
        tall = jnp.concatenate([value[:, b * taps : (b + 1) * taps] for b in range(blocks)], axis=0)
        return jnp.concatenate([tall, tall], axis=1)

    spec_x[...] = mm(stacked(trace_rows), twice)
    spec_t[...] = mm(stacked(target_rows), twice)
    sign = 1.0 - 2.0 * (iota((16, taps), 1) & 1).astype(F32)
    out = []
    for start in range(0, rows, 16):
        c0r = c0i = c1r = c1i = p0 = p1r = p1i = jnp.zeros((16, taps), F32)
        xr0 = xi0 = None
        for b in range(blocks):
            here = pl.ds(b * rows + start, 16)
            xr, xi = spec_x[here, :taps], spec_x[here, taps:]
            tr, ti = spec_t[here, :taps], spec_t[here, taps:]
            c0r += xr * tr + xi * ti
            c0i += xr * ti - xi * tr
            p0 += xr * xr + xi * xi
            if b:
                c1r += xr0 * tr + xi0 * ti
                c1i += xr0 * ti - xi0 * tr
                p1r += xr0 * xr + xi0 * xi
                p1i += xr0 * xi - xi0 * xr
            xr0, xi0 = xr, xi
        power = jnp.sum(p0, axis=1, keepdims=True) * (1.0 / taps)
        out.append(
            (
                jnp.concatenate([p0 + sign * p1i, -sign * p1r], axis=1),
                jnp.concatenate([c0r + sign * c1i, c0i - sign * c1r], axis=1),
                jnp.concatenate([xr0, xi0], axis=1),
                jnp.broadcast_to(power, (16, 128)),
            )
        )
    auto, cross, last, power = (jnp.concatenate(parts, axis=0) for parts in zip(*out))
    return fine_mm(auto, even), cross, last, power


def gradients(mixed, q, cross, last, twice, tail, inverse):
    taps = q.shape[1]
    fs = mm(jnp.concatenate([mixed, mixed], axis=1), twice)
    fr, fi = fs[:, :taps], fs[:, taps:]
    xr, xi = last[:, :taps], last[:, taps:]
    over = fine_mm(jnp.concatenate([xr * fr - xi * fi, xr * fi + xi * fr], axis=1), tail)
    yr, yi = over[:, :taps], over[:, taps:]
    gr = q * fr - cross[:, :taps] - (xr * yr + xi * yi)
    gi = q * fi - cross[:, taps:] - (xr * yi - xi * yr)
    return fine_mm(jnp.concatenate([gr, gi], axis=1), inverse)


def settled_src(filters, here, grads, energy):
    missing = jnp.zeros((8 - filters.shape[0], filters.shape[1]), F32)
    sums = pick_mm(here, split2(grads))
    return jnp.concatenate([filters, missing], axis=0) - STEP * sums / jnp.maximum(energy, 1.0)


def src_rows(here, src_filters):
    missing = jnp.zeros((8 - src_filters.shape[0], src_filters.shape[1]), F32)
    return folded(mm_t(here, split2(jnp.concatenate([src_filters, missing], axis=0))))


def fused_kernel(
    sizes, counts, traces, targets, src_row, rcv_row, cmp_row, rcv_home, cmp_home,
    src_f, rcv_f, cmp_f, twice, even, tail, inverse,
    out,
    v_traces, v_targets, v_src_row, v_rcv_row, v_cmp_row, v_rcv_home, v_cmp_home,
    v_src_f, v_twice, v_even, v_tail, v_inverse,
    table, req_send, req_recv, vals, fetched, hot, grad_send, grad_recv, part, inbox,
    mixed, slot_hot, slot_hot_t, q, cross, last, power, spec_x, spec_t,
    local_sem, req_ss, req_rs, tab_ss, tab_rs, val_ss, val_rs, grad_ss, grad_rs, part_ss, part_rs,
):
    lines, plane, slot_cap, terms = sizes
    rcv_terms, cmp_terms = terms
    rows_all = rcv_terms + cmp_terms
    pair = 2 * slot_cap
    width = plane * pair
    count = v_traces.shape[0]
    me = lax.axis_index("shot") * lines + lax.axis_index("line")
    z, p = me // plane, me % plane

    def device(index):
        return (index // lines, index % lines)

    def peer(offset):
        return (p + offset) % plane

    def remote(source, target, send, recv, index):
        return pltpu.make_async_remote_copy(
            src_ref=source, dst_ref=target, send_sem=send, recv_sem=recv,
            device_id=device(index), device_id_type=pl.DeviceIdType.MESH,
        )

    barrier = pltpu.get_barrier_semaphore()

    def greet(index):
        pl.semaphore_signal(barrier, inc=1, device_id=device(index), device_id_type=pl.DeviceIdType.MESH)

    for distance in range(1, Z):
        greet((z + distance) % Z * plane + p)
    for offset in range(1, plane):
        greet(z * plane + peer(offset))

    small = [
        (rcv_row, v_rcv_row), (cmp_row, v_cmp_row), (rcv_home, v_rcv_home), (cmp_home, v_cmp_home),
        (rcv_f, table.at[z, pl.ds(0, rcv_terms)]), (cmp_f, table.at[z, pl.ds(rcv_terms, cmp_terms)]),
        (src_row, v_src_row), (src_f, v_src_f), (even, v_even), (inverse, v_inverse),
        (traces, v_traces), (targets, v_targets),
    ]
    for source, target in ((twice, v_twice), (tail, v_tail)):
        high = target.shape[0]
        small += [(source.at[pl.ds(i * high, high)], target.at[:, pl.ds(i * 128, 128)]) for i in range(2)]
    copies = [
        pltpu.make_async_copy(source, target, local_sem.at[i]) for i, (source, target) in enumerate(small)
    ]
    for copy in copies:
        copy.start()
    pl.semaphore_wait(barrier, plane - 1 + Z - 1)

    share = rows_all // PIECES

    def table_copy(way, distance, piece):
        chunk = z - distance if way == 0 else z + distance
        target = me + plane if way == 0 else me - plane
        rows = table.at[chunk, pl.ds(piece * share, share)]
        return remote(
            rows, rows, tab_ss.at[way, distance, piece], tab_rs.at[way, distance + 1, piece], target
        )

    def table_wait(way, distance, piece):
        chunk = z - distance if way == 0 else z + distance
        rows = table.at[chunk, pl.ds(piece * share, share)]
        remote(
            rows, rows, tab_ss.at[way, distance, piece], tab_rs.at[way, distance, piece], me
        ).wait_recv()

    def arrives(way, distance):
        return z >= distance if way == 0 else z <= Z - 1 - distance

    def goes_on(way, distance):
        return ((z >= distance) & (z < Z - 1)) if way == 0 else ((z <= Z - 1 - distance) & (z > 0))

    copies[4].wait()
    copies[5].wait()
    for piece in range(PIECES):
        for way in range(2):
            pl.when(goes_on(way, 0))(lambda way=way, piece=piece: table_copy(way, 0, piece).start())
    for i in range(4):
        copies[i].wait()

    found = [
        find_slots(v_rcv_row[...], v_rcv_home[...], rcv_terms),
        find_slots(v_cmp_row[...], v_cmp_home[...], cmp_terms),
    ]
    lane = iota((count, 128), 1)
    req_rows = 2 * Z * plane
    req_iota = iota((req_rows, count), 0)
    wanted = ((req_iota >> 1) & (Z - 1)) * plane + req_iota // (2 * Z)
    slots, slot_rows, owner_rows, rank_hots = [], [], [], []
    request = jnp.zeros((req_rows, 128), F32)
    for kind, (owner, rank, place) in enumerate(found):
        owner_row = as_row(owner)
        slot = owner * pair + (kind * slot_cap + rank)
        rank_hot = lane == rank
        lhs = pick_mask((wanted == owner_row) & ((req_iota & 1) == kind))
        request = request + mm(lhs, jnp.where(rank_hot, place, 0.0).astype(BF))
        slots.append(slot)
        slot_rows.append(as_row(slot))
        owner_rows.append(owner_row)
        rank_hots.append(rank_hot)
    req_send[...] = request.reshape(plane, 2 * Z, 128)
    req_copies = [
        remote(
            req_send.at[peer(offset)], req_recv.at[p], req_ss.at[offset], req_rs.at[p],
            z * plane + peer(offset),
        )
        for offset in range(1, plane)
    ]
    for copy in req_copies:
        copy.start()
    req_recv[pl.ds(p, 1)] = req_send[pl.ds(p, 1)]

    for i in range(6, 16):
        copies[i].wait()

    def spectra(start, stop):
        @pl.loop(start, stop)
        def _(turn):
            here = pl.ds(pl.multiple_of(turn * ROWS, ROWS), ROWS)
            q[here, :], cross[here, :], last[here, :], power[here, :] = spectra_rows(
                v_traces[here, :], v_targets[here, :], v_twice[...], v_even[...], spec_x, spec_t
            )

    turns = count // ROWS
    spectra(0, turns // 4)

    for offset in range(1, plane):
        source = peer(offset)
        remote(
            req_send.at[source], req_recv.at[source], req_ss.at[offset], req_rs.at[source], me
        ).wait_recv()

    cap_bits = slot_cap.bit_length() - 1

    def value_copy(chunk, offset):
        return remote(
            vals.at[chunk, peer(offset)], fetched.at[chunk, p], val_ss.at[chunk, offset],
            val_rs.at[chunk, p], z * plane + peer(offset),
        )

    def serve(chunk):
        request_rows = req_recv[...].reshape(plane * 2 * Z, 128).astype(BF)
        row = iota((width, plane * 2 * Z), 0)
        col = iota((width, plane * 2 * Z), 1)
        kind = (row >> cap_bits) & 1
        expand = pick_mask(col == (row >> (cap_bits + 1)) * (2 * Z) + 2 * chunk + kind)
        wide = mm(expand, request_rows)
        row = iota((width, 128), 0)
        mine = (row & (slot_cap - 1)) == iota((width, 128), 1)
        place = mm(jnp.where(mine, wide, 0.0).astype(BF), jnp.ones((128, 128), BF)).astype(jnp.int32)
        place = place + ((row >> cap_bits) & 1) * rcv_terms
        onehot = jnp.concatenate(
            [pick_mask(iota((width, 128), 1) + base == place) for base in range(0, rows_all, 128)], axis=1
        )
        vals[chunk] = pick_mm(onehot, split2(table[chunk])).reshape(plane, pair, 128)
        for offset in range(1, plane):
            value_copy(chunk, offset).start()
        fetched[chunk, pl.ds(p, 1)] = vals[chunk, pl.ds(p, 1)]
        hot[chunk] = pick_mask(iota((rows_all, width), 0) == as_row(place))

    def take(chunk):
        for offset in range(1, plane):
            source = peer(offset)
            remote(
                vals.at[chunk, source], fetched.at[chunk, source], val_ss.at[chunk, offset],
                val_rs.at[chunk, source], me,
            ).wait_recv()
        mixed[...] += pick_mm(slot_hot[chunk], split2(fetched[chunk].reshape(width, 128)))

    serve(z)
    src_hot = pick_mask(iota((8, count), 0) == v_src_row[...])
    mixed[...] = src_rows(src_hot, v_src_f[...])

    def near(act, distance):
        if distance == 0:
            act(z)
            return
        for way in range(2):
            chunk = z - distance if way == 0 else z + distance
            pl.when(arrives(way, distance))(lambda chunk=chunk: act(chunk))

    marks = [turns // 4, 5 * turns // 8, turns, turns]
    for distance in range(1, Z):
        for piece in range(PIECES):
            for way in range(2):
                pl.when(arrives(way, distance))(lambda way=way, piece=piece: table_wait(way, distance, piece))
                if distance < Z - 1:
                    pl.when(goes_on(way, distance))(
                        lambda way=way, piece=piece: table_copy(way, distance, piece).start()
                    )
        near(serve, distance)
        if distance == 1:
            for chunk in range(Z):
                slot_hot[chunk] = both_hot(slots, chunk * width, width)
        spectra(marks[distance - 1], marks[distance])
        if distance == 2:
            powers = jnp.where(iota((count, 128), 0) < counts[0], power[...], 0.0)
            row = iota((Z * plane * 8, count), 0)
            energy = jnp.zeros((Z * plane * 8, 128), F32)
            for kind in range(2):
                onehot = pick_mask(((row >> 3) == owner_rows[kind]) & ((row & 7) == kind))
                energy = energy + pick_mm(onehot, split2(jnp.where(rank_hots[kind], powers, 0.0)))
            grad_send[:, :, pl.ds(pair, 8), :] = energy.reshape(Z, plane, 8, 128)
            src_energy = pick_mm(src_hot, split2(powers))
            for chunk in range(Z):
                row = iota((width, count), 0) + chunk * width
                slot_hot_t[chunk] = pick_mask((row == slot_rows[0]) | (row == slot_rows[1]))
        near(take, distance - 1)
    near(take, Z - 1)

    grads = gradients(
        mixed[...].astype(BF), q[...], cross[...], last[...], v_twice[...], v_tail[...], v_inverse[...]
    )
    grads = jnp.where(iota((count, 128), 0) < counts[0], grads, 0.0)
    grad_parts = split2(grads)

    order = (3 * (1 - z // 2), (2 + 3 * z) % 5, 1 + z % 2, z)

    def grad_copy(chunk, offset):
        return remote(
            grad_send.at[chunk, peer(offset)], grad_recv.at[chunk, p], grad_ss.at[chunk, offset],
            grad_rs.at[chunk, p], z * plane + peer(offset),
        )

    for chunk in order:
        sent = pick_mm(slot_hot_t[chunk], grad_parts)
        grad_send[chunk, :, pl.ds(0, pair), :] = sent.reshape(plane, pair, 128)
        for offset in range(1, plane):
            grad_copy(chunk, offset).start()
        grad_recv[chunk, pl.ds(p, 1)] = grad_send[chunk, pl.ds(p, 1)]
    out[pl.ds(rows_all, 8)] = settled_src(v_src_f[...], src_hot, grads, src_energy)

    spans = [pl.ds(i * share, share + (8 if i == PIECES - 1 else 0)) for i in range(PIECES)]

    def part_copy(chunk, way, piece):
        target = me + plane if way == 0 else me - plane
        rows = spans[piece]
        return remote(
            part.at[chunk, rows], inbox.at[way, chunk, rows], part_ss.at[chunk, piece],
            part_rs.at[way, chunk, piece], target,
        )

    def add_inbox(chunk, way, piece):
        rows = spans[piece]
        remote(
            part.at[chunk, rows], inbox.at[way, chunk, rows], part_ss.at[chunk, piece],
            part_rs.at[way, chunk, piece], me,
        ).wait_recv()
        part[chunk, rows] = part[chunk, rows] + inbox[way, chunk, rows]

    def relay(chunk, way, add):
        for piece in range(PIECES):
            if add:
                add_inbox(chunk, way, piece)
            part_copy(chunk, way, piece).start()

    for step, chunk in enumerate(order):
        for offset in range(1, plane):
            source = peer(offset)
            remote(
                grad_send.at[chunk, source], grad_recv.at[chunk, source], grad_ss.at[chunk, offset],
                grad_rs.at[chunk, source], me,
            ).wait_recv()
        onehot = hot[chunk]
        got = split2(grad_recv[chunk, :, pl.ds(0, pair), :].reshape(width, 128))
        part[chunk, pl.ds(0, rows_all)] = pick_mm(onehot, got)
        energy = grad_recv[chunk, :, pl.ds(pair, 8), :].reshape(plane * 8, 128)
        row, col = iota((plane * 8, width), 0), iota((plane * 8, width), 1)
        spread = pick_mask(
            ((row >> 3) == (col >> (cap_bits + 1))) & ((row & 7) == ((col >> cap_bits) & 1))
        )
        wide = mm_t(split2(energy), spread)
        mine = (iota((256, width), 1) & (slot_cap - 1)) == (iota((256, width), 0) & 127)
        energy = jnp.sum(jnp.where(mine, wide, 0.0), axis=0, keepdims=True)
        high = energy.astype(BF).astype(F32)
        energy = jnp.where(iota((8, width), 0) < 4, high, energy - high).astype(BF)
        energy = lax.dot_general(energy, onehot, (((1,), (1,)), ((), ())), preferred_element_type=F32)
        energy = energy[0:1] + energy[4:5]
        lines8 = iota((8, 128), 0)
        packed = jnp.zeros((8, 128), F32)
        for i in range(rows_all // 128):
            packed = packed + jnp.where(lines8 == i, energy[:, i * 128 : (i + 1) * 128], 0.0)
        part[chunk, pl.ds(rows_all, 8)] = packed
        if step < Z - 1:
            pl.when((chunk > z) & (z == 0))(lambda chunk=chunk: relay(chunk, 0, False))
            pl.when((chunk < z) & (z == Z - 1))(lambda chunk=chunk: relay(chunk, 1, False))
        if step:
            before = order[step - 1]
            pl.when((before > z) & (z > 0))(lambda before=before: relay(before, 0, True))
            pl.when((before < z) & (z < Z - 1))(lambda before=before: relay(before, 1, True))
    for piece in range(PIECES):
        pl.when(z > 0)(lambda piece=piece: add_inbox(z, 0, piece))
        pl.when(z < Z - 1)(lambda piece=piece: add_inbox(z, 1, piece))

    packed = part[z, pl.ds(rows_all, 8)]
    for i in range(rows_all // 128):
        energy = jnp.transpose(jnp.broadcast_to(packed[i : i + 1, :], (128, 128)))
        here = pl.ds(i * 128, 128)
        updated = table[z, here] - STEP * part[z, here] / jnp.maximum(energy, 1.0)
        out[here, :] = updated

    for copy in req_copies:
        copy.wait_send()
    for distance in range(Z - 1):
        for way in range(2):
            for piece in range(PIECES):
                pl.when(goes_on(way, distance))(
                    lambda way=way, piece=piece: table_copy(way, distance, piece).wait_send()
                )
    for chunk in range(Z):
        for offset in range(1, plane):
            value_copy(chunk, offset).wait_send()
            grad_copy(chunk, offset).wait_send()
        for piece in range(PIECES):
            pl.when(z != chunk)(lambda chunk=chunk, piece=piece: part_copy(chunk, 0, piece).wait_send())


def deliver_kernel(updated, src_out, rcv_out, cmp_out, held, sems):
    rcv_terms, cmp_terms = rcv_out.shape[0], cmp_out.shape[0]
    spans = (
        (rcv_terms + cmp_terms, src_out.shape[0], src_out),
        (0, rcv_terms, rcv_out),
        (rcv_terms, cmp_terms, cmp_out),
    )
    loads, stores = [], []
    for i, (start, size, target) in enumerate(spans):
        padded = (size + 7) // 8 * 8
        loads.append(
            pltpu.make_async_copy(updated.at[pl.ds(start, padded)], held.at[pl.ds(start, padded)], sems.at[0, i])
        )
        stores.append(pltpu.make_async_copy(held.at[pl.ds(start, size)], target, sems.at[1, i]))
    for load in loads:
        load.start()
    for load, store in zip(loads, stores):
        load.wait()
        store.start()
    for store in stores:
        store.wait()


def body(
    traces, targets, src_local, rcv_term, cmp_term, rcv_home, cmp_home, counts,
    src_filters, rcv_filters, cmp_filters,
):
    trace_rows, samples = traces.shape
    taps = src_filters.shape[1]
    device_count = lax.axis_size(AXES)
    lines = lax.axis_size("line")
    slot_cap = max(2, 2 * trace_rows // device_count)
    plane = device_count // Z
    pair = 2 * slot_cap
    blocks = samples // taps
    terms = (rcv_filters.shape[0], cmp_filters.shape[0])
    rows_all = sum(terms)
    tables = tuple(jnp.asarray(table) for table in spectral_tables(taps))
    shape = jax.ShapeDtypeStruct
    vmem, sem = pltpu.VMEM, pltpu.SemaphoreType.DMA
    operands = (
        traces, targets, src_local.reshape(1, -1), rcv_term.reshape(1, -1), cmp_term.reshape(1, -1),
        rcv_home.reshape(-1, 128), cmp_home.reshape(-1, 128),
        src_filters, rcv_filters, cmp_filters, *tables,
    )
    held = [vmem(x.shape, x.dtype) for x in operands[:8]]
    held += [vmem((x.shape[0] * 128 // w, w), x.dtype) for x, w in zip(tables, (256, 128, 256, 128))]
    updated = pl.pallas_call(
        functools.partial(fused_kernel, (lines, plane, slot_cap, terms)),
        out_shape=shape((rows_all + 8, taps), F32),
        in_specs=[pl.BlockSpec(memory_space=pltpu.SMEM)]
        + [pl.BlockSpec(memory_space=pltpu.HBM)] * len(operands),
        out_specs=pl.BlockSpec(memory_space=pltpu.VMEM),
        scratch_shapes=held
        + [
            vmem((Z, rows_all, 128), F32),
            vmem((plane, 2 * Z, 128), F32),
            vmem((plane, 2 * Z, 128), F32),
            vmem((Z, plane, pair, 128), F32),
            vmem((Z, plane, pair, 128), F32),
            vmem((Z, rows_all, plane * pair), BF),
            vmem((Z, plane, pair + 8, 128), F32),
            vmem((Z, plane, pair + 8, 128), F32),
            vmem((Z, rows_all + 8, 128), F32),
            vmem((2, Z, rows_all + 8, 128), F32),
            vmem((trace_rows, taps), F32),
            vmem((Z, trace_rows, plane * pair), BF),
            vmem((Z, plane * pair, trace_rows), BF),
            vmem((trace_rows, taps), F32),
            vmem((trace_rows, 2 * taps), F32),
            vmem((trace_rows, 2 * taps), F32),
            vmem((trace_rows, 128), F32),
            vmem((ROWS * blocks, 2 * taps), F32),
            vmem((ROWS * blocks, 2 * taps), F32),
            sem((16,)),
            sem((plane,)), sem((plane,)),
            sem((2, Z, PIECES)), sem((2, Z + 1, PIECES)),
            sem((Z, plane)), sem((Z, plane)),
            sem((Z, plane)), sem((Z, plane)),
            sem((Z, PIECES)), sem((2, Z, PIECES)),
        ],
        compiler_params=pltpu.CompilerParams(
            vmem_limit_bytes=VMEM_LIMIT, collective_id=0, has_side_effects=True
        ),
        cost_estimate=pl.CostEstimate(
            flops=16 * trace_rows * samples * taps, bytes_accessed=6 * 2**20, transcendentals=0
        ),
    )(counts, *operands)
    anywhere = pl.BlockSpec(memory_space=pl.ANY)
    return pl.pallas_call(
        deliver_kernel,
        out_shape=tuple(shape(x.shape, F32) for x in (src_filters, rcv_filters, cmp_filters)),
        in_specs=[anywhere],
        out_specs=(anywhere,) * 3,
        scratch_shapes=[vmem((rows_all + 8, taps), F32), sem((2, 3))],
        compiler_params=pltpu.CompilerParams(vmem_limit_bytes=VMEM_LIMIT),
    )(updated)


def solution(mesh):
    rows, flat = P(AXES, None), P(AXES)
    return jax.shard_map(
        body,
        mesh=mesh,
        in_specs=(rows, rows, flat, flat, flat, P(), P(), flat, rows, rows, rows),
        out_specs=(rows, rows, rows),
        check_vma=False,
    )
```
